32 devices in a mesh: seq: 4 (over x, core), head: 8 (over z, y).
Axes of the slice: x: 2, y: 2, z: 4, core: 2. Of those that a mesh axis runs over, the one named last changes fastest.
Arguments:
- x_inner: bfloat16 [6144, 16384], P('seq', 'head'), may hold values from -400 to 400
- z_gate: bfloat16 [6144, 16384], P('seq', 'head'), may hold values from -6 to 6
- bc_raw: bfloat16 [6144, 512], P(('seq', 'head')), may hold values from -6 to 6
- conv_weight: float32 [4, 512], replicated, may hold values from -3 to 3
- conv_bias: float32 [512], replicated, may hold values from -3 to 3
- dt_raw: float32 [6144, 128], P('seq', 'head'), may hold values from -6 to 6144
- a_log: float32 [128], P('head'), may hold values from -20 to 1
- d_skip: float32 [128], P('head'), may hold values from 0.5 to 1.5
- norm_gain: float32 [16384], P('head'), may hold values from 0.5 to 1.5
Outputs:
- mixer_out: bfloat16 [6144, 16384], P('seq', 'head')
The draws below stay inside these ranges and needn't reach their ends.
All inputs are finite; a program needn't handle non-finite values.
Results may differ from the reference program's by a relative error of at most 0.0034.
Values may be sent and summed in bfloat16 or wider, within the bound.
No kernel may reach another device: no remote copies, remote signals or barrier semaphores. Data moves between devices by JAX's collectives and lax.ppermute only.
A program may use at most 128 MiB of HBM per device.

```python
import math
import jax
import jax.numpy as jnp
from jax import lax

HEADS = 128
HEAD_DIM = 128
STATE = 256
CONV = 4
BLOCK = 256
SEQ_DEV = 1536
TOKENS = 6144
INNER = 16384


def decay_rates(key):
    subkeys = jax.random.split(jax.random.fold_in(key, 7), 6)
    quick_share = 0.5
    fast_flags = jax.random.uniform(subkeys[0], (HEADS,)) < quick_share
    jitter = jax.random.uniform(subkeys[1], (HEADS,), minval=-0.15, maxval=0.15)
    slow_rate = 0.3 / (TOKENS * 0.05)
    velocity_values = jnp.where(fast_flags, 0.5, slow_rate) * jnp.exp(jitter)
    roughness = jax.random.uniform(subkeys[2], (TOKENS, HEADS), minval=0.5, maxval=1.5)
    blocks = jnp.exp(jax.random.uniform(subkeys[3], (TOKENS // SEQ_DEV, HEADS), minval=-0.7, maxval=0.7))
    delta_widths = 0.05 * roughness * jnp.repeat(blocks, SEQ_DEV, axis=0)
    places = jax.random.randint(subkeys[4], (HEADS, 3), 0, TOKENS)
    penalty_terms = jax.random.uniform(subkeys[5], (HEADS, 3), minval=0.22, maxval=0.51)
    agreement_flags = (jnp.arange(TOKENS)[:, None, None] == places[None]).astype(jnp.float32)
    spike_penalty = jnp.sum(agreement_flags * penalty_terms[None], axis=2)
    flagged_entries = (spike_penalty > 0.0) & jnp.logical_not(fast_flags)[None, :]
    delta_widths = jnp.where(flagged_entries, spike_penalty / velocity_values[None, :], delta_widths)
    return (velocity_values, delta_widths, flagged_entries)


def draw_a_log(key, part):
    velocity_values, delta_widths, flagged_entries = decay_rates(key)
    return jnp.log(velocity_values).astype(jnp.float32)


def draw_dt_raw(key, part):
    velocity_values, delta_widths, flagged_entries = decay_rates(key)
    return (delta_widths + jnp.log(-jnp.expm1(-delta_widths))).astype(jnp.float32)


def draw_x_inner(key, part):
    velocity_values, delta_widths, flagged_entries = decay_rates(key)
    subkeys = jax.random.split(jax.random.fold_in(key, 11), 3)
    values = jnp.clip(jax.random.normal(subkeys[0], (TOKENS, INNER), jnp.float32), -4.0, 4.0)
    channel_scale = jnp.exp(jax.random.uniform(subkeys[1], (INNER,), minval=0.0, maxval=math.log(10.0)))
    token_scale = jnp.exp(jax.random.uniform(subkeys[2], (TOKENS, 1), minval=0.0, maxval=math.log(10.0)))
    rise_base = 3.0
    head_rise = rise_base ** ((jnp.arange(INNER) // HEAD_DIM).astype(jnp.float32) / HEADS)
    damping = jnp.repeat(jnp.where(flagged_entries, 0.05 / delta_widths, 1.0), HEAD_DIM, axis=1)
    return (values * channel_scale[None, :] * head_rise[None, :] * token_scale * damping / 10.0).astype(jnp.bfloat16)


def level_of(key, extent, shards, low, high):
    gain = 1.0
    for dim, blocks in shards:
        draws = jax.random.uniform(jax.random.fold_in(jax.random.fold_in(key, 6), dim), (blocks,), jnp.float32, low / len(shards), high / len(shards))
        gain = gain * jnp.repeat(jnp.exp(draws), extent[dim] // blocks).reshape((-1,) + (1,) * (len(extent) - 1 - dim))
    return gain


def noise(own_key, extent, scale, most, pieces=(), kind=jnp.bfloat16):
    array = jax.random.normal(own_key, extent, jnp.float32) * scale
    if len(pieces) > 0:
        array = level_of(own_key, extent, pieces, -0.22, 0.18) * array
    return jnp.clip(array, min=-most, max=most).astype(kind)


def setup_inputs(seed: int = 0) -> dict:
    keys = jax.random.split(jax.random.key(seed), 10)
    x_inner = draw_x_inner(jax.random.fold_in(keys[9], 71), 0)
    z_gate = noise(keys[1], (TOKENS, INNER), 1.0, 6.0, ((0, 4), (1, 8)))
    bc_raw = noise(keys[2], (TOKENS, 2 * STATE), 1.0, 6.0, ((0, 32),))
    conv_weight = noise(keys[3], (CONV, 2 * STATE), CONV ** -0.5, 3.0, (), jnp.float32)
    conv_bias = noise(keys[4], (2 * STATE,), 0.5, 3.0, (), jnp.float32)
    dt_raw = draw_dt_raw(jax.random.fold_in(keys[9], 71), 0)
    a_log = draw_a_log(jax.random.fold_in(keys[9], 71), 0)
    d_skip = jnp.clip(0.5 + 1.0 * jax.random.uniform(keys[7], (HEADS,), jnp.float32) ** level_of(keys[7], (HEADS,), ((0, 8),), -0.2, 0.2), 0.5, 1.5)
    norm_gain = jnp.clip(1.0 + 0.1 * jax.random.normal(keys[8], (INNER,), jnp.float32), 0.5, 1.5)
    return dict(x_inner=x_inner, z_gate=z_gate, bc_raw=bc_raw, conv_weight=conv_weight, conv_bias=conv_bias, dt_raw=dt_raw, a_log=a_log, d_skip=d_skip, norm_gain=norm_gain)


def convolve_rows(bc_raw, conv_weight, conv_bias):
    tap_count = conv_weight.shape[0]
    row_count = bc_raw.shape[0]
    padded = jnp.concatenate([jnp.zeros((tap_count - 1, bc_raw.shape[1]), jnp.float32), bc_raw.astype(jnp.float32)], axis=0)
    accumulated = jnp.broadcast_to(conv_bias[None, :], (row_count, bc_raw.shape[1]))
    for offset in range(tap_count):
        accumulated = accumulated + conv_weight[offset][None, :] * padded[offset:offset + row_count]
    return jax.nn.silu(accumulated).astype(jnp.bfloat16)

def reference(x_inner, z_gate, bc_raw, conv_weight, conv_bias, dt_raw, a_log, d_skip, norm_gain):
    bc_act = convolve_rows(bc_raw, conv_weight, conv_bias)
    step_size = jax.nn.softplus(dt_raw)
    log_step = -jnp.exp(a_log)[None, :] * step_size
    block_count = TOKENS // BLOCK
    inputs = (x_inner.reshape(block_count, BLOCK, HEADS, HEAD_DIM), z_gate.reshape(block_count, BLOCK, INNER), bc_act.reshape(block_count, BLOCK, 2 * STATE), log_step.reshape(block_count, BLOCK, HEADS), step_size.reshape(block_count, BLOCK, HEADS))
    lower_mask = jnp.tril(jnp.ones((BLOCK, BLOCK), dtype=bool))
    highest = lax.Precision.HIGHEST

    def advance(carried, block_inputs):
        x_block, z_block, bc_block, log_block, size_block = block_inputs
        b_float = bc_block[:, :STATE].astype(jnp.float32)
        c_float = bc_block[:, STATE:].astype(jnp.float32)
        cum_log = jnp.cumsum(log_block, axis=0)
        gram_matrix = jnp.dot(bc_block[:, STATE:], bc_block[:, :STATE].T, preferred_element_type=jnp.float32)
        by_head = cum_log.T
        spread = by_head[:, :, None] - by_head[:, None, :]
        decay_blocks = jnp.where(lower_mask[None], jnp.exp(jnp.where(lower_mask[None], spread, 0.0)), 0.0)
        weights = gram_matrix[None] * decay_blocks * size_block.T[:, None, :]
        x_float = x_block.astype(jnp.float32)
        inner_part = jnp.einsum('hij,jhp->ihp', weights, x_float, precision=highest)
        carried_part = jnp.exp(cum_log)[:, :, None] * jnp.einsum('in,hpn->ihp', c_float, carried, precision=highest)
        tail_weight = jnp.exp(cum_log[-1][None, :] - cum_log) * size_block
        updated = jnp.exp(cum_log[-1])[:, None, None] * carried + jnp.einsum('jhp,jn->hpn', x_float * tail_weight[:, :, None], b_float, precision=highest)
        ssm_out = inner_part + carried_part + d_skip[None, :, None] * x_float
        gated_out = ssm_out.reshape(BLOCK, INNER) * jax.nn.silu(z_block.astype(jnp.float32))
        inverse_rms = lax.rsqrt(lax.optimization_barrier(jnp.sum(gated_out * gated_out, axis=1, keepdims=True)) / INNER + 1e-05)
        return (updated, (gated_out * inverse_rms * norm_gain[None, :]).astype(jnp.bfloat16))
    initial = jnp.zeros((HEADS, HEAD_DIM, STATE), jnp.float32)
    final_state, blocks = lax.scan(advance, initial, inputs)
    return blocks.reshape(TOKENS, INNER)
```

```python
import functools
import math

import jax
import jax.numpy as jnp
from jax import lax
from jax.experimental import pallas as pl
from jax.experimental.pallas import tpu as pltpu
from jax.sharding import PartitionSpec as P

HEAD_DIM = 128
STATE = 256
BLOCK = 256
INNER = 16384
RIM = 16
SLOT = 16
LOG2E = math.log2(math.e)
F32 = jnp.float32
BF16 = jnp.bfloat16
HIGHEST = lax.Precision.HIGHEST
VMEM_LIMIT = 48 * 1024 * 1024


def params():
    return pltpu.CompilerParams(vmem_limit_bytes=VMEM_LIMIT)


def whole(memory_space=pltpu.VMEM):
    return pl.BlockSpec(memory_space=memory_space)


def cost(flops, nbytes, trans=0):
    return pl.CostEstimate(flops=int(flops), bytes_accessed=int(nbytes), transcendentals=int(trans))


def silu(v):
    half = 0.5 * v
    return half + half * jnp.tanh(half)


def split(v):
    high = v.astype(BF16).astype(F32)
    return high, v - high


def conv_slab(slab, weight, bias):
    taps = weight.shape[0]
    total = jnp.broadcast_to(bias, slab.shape)
    for k in range(taps):
        shift = taps - 1 - k
        moved = pltpu.roll(slab, shift, 0) if shift else slab
        total = total + weight[k : k + 1, :] * moved
    total = total[RIM:]
    return (total * jax.nn.sigmoid(total)).astype(BF16)


def rates_kernel(dt_ref, a_ref, q_ref, b_ref, ends_ref):
    block_count = dt_ref.shape[1] // BLOCK
    rate = -jnp.exp(a_ref[...])
    upper = (
        lax.broadcasted_iota(jnp.int32, (BLOCK, BLOCK), 0)
        <= lax.broadcasted_iota(jnp.int32, (BLOCK, BLOCK), 1)
    ).astype(F32)
    prior = jnp.zeros((SLOT, 1), F32)
    lane = lax.broadcasted_iota(jnp.int32, (SLOT, 128), 1)
    ends = jnp.zeros((SLOT, 128), F32)
    for c in range(block_count):
        columns = slice(c * BLOCK, (c + 1) * BLOCK)
        dt = dt_ref[:, columns]
        step = jnp.maximum(dt, 0.0) + jnp.log1p(jnp.exp(-jnp.abs(dt)))
        cum = jnp.dot(rate * step, upper, precision=HIGHEST, preferred_element_type=F32)
        last = cum[:, BLOCK - 1 : BLOCK]
        scaled = cum * LOG2E
        b_ref[:, columns] = scaled - jnp.log(step) * LOG2E
        parts = [scaled]
        parts.extend(split(jnp.exp(last - cum) * step))
        parts.extend(split(jnp.exp(cum)))
        parts.extend(split(jnp.exp(cum + prior)))
        parts.append(jnp.zeros_like(cum))
        q_ref[columns, :] = jnp.concatenate(parts, axis=0).T
        ends = jnp.where(lane == c, last, ends)
        prior = prior + last
    ends_ref[...] = ends


def rates(dt, a_log):
    length = dt.shape[1]
    return pl.pallas_call(
        rates_kernel,
        out_shape=[
            jax.ShapeDtypeStruct((length, 128), F32),
            jax.ShapeDtypeStruct((SLOT, length), F32),
            jax.ShapeDtypeStruct((SLOT, 128), F32),
        ],
        in_specs=[whole()] * 2,
        out_specs=[whole()] * 3,
        compiler_params=params(),
        cost_estimate=cost(12 * 2 * SLOT * BLOCK * length, 1 << 20),
    )(dt, a_log)


def expander(ref, slot):
    row = lax.broadcasted_iota(jnp.int32, ref.shape, 0)
    head = lax.broadcasted_iota(jnp.int32, ref.shape, 1) // HEAD_DIM
    ref[...] = ((row == slot * SLOT + head) | (row == (slot + 1) * SLOT + head)).astype(BF16)


def act_kernel(own_rows, zone_count, me_ref, own_ref, *refs):
    zones = refs[: zone_count - 1]
    side_ref, others_ref, rim_ref, weight_ref, bias_ref, act_ref, first_ref, last_ref, raw = refs[
        zone_count - 1 :
    ]
    me = me_ref[0]
    size = 2 * zone_count
    per = own_ref.shape[0]

    def place(owner, ref, start):
        at = pl.multiple_of(RIM + owner * own_rows, 16)
        raw[pl.ds(at, own_rows), :] = ref[start : start + own_rows, :]

        @pl.when(owner == size - 1)
        def _():
            last_ref[0:RIM, :] = ref[start + own_rows - RIM : start + own_rows, :]
            if per > own_rows:
                last_ref[RIM : 2 * RIM, :] = ref[start + own_rows : start + own_rows + RIM, :]

    raw[0:RIM, :] = rim_ref[...]
    place(me, own_ref, 0)
    partner = me + 1 - 2 * lax.rem(me, 2)
    place(partner, side_ref, 0)
    for k in range(1, zone_count):
        place(lax.rem(me - 2 * k + size, size), zones[k - 1], 0)
        place(lax.rem(partner - 2 * k + size, size), others_ref, (k - 1) * per)
    first_ref[...] = raw[RIM : 2 * RIM, :]
    weight = weight_ref[...]
    bias = bias_ref[...]
    for c in range(act_ref.shape[0] // BLOCK):
        slab = raw[c * BLOCK : c * BLOCK + RIM + BLOCK, :].astype(F32)
        act_ref[c * BLOCK : (c + 1) * BLOCK, :] = conv_slab(slab, weight, bias)


def activate(me, own, zones, side, others, rim, weight, bias, own_rows):
    zone_count = len(zones) + 1
    length = 2 * zone_count * own_rows
    columns = own.shape[1]
    return pl.pallas_call(
        functools.partial(act_kernel, own_rows, zone_count),
        out_shape=[
            jax.ShapeDtypeStruct((length, columns), BF16),
            jax.ShapeDtypeStruct((RIM, columns), BF16),
            jax.ShapeDtypeStruct((2 * RIM, columns), BF16),
        ],
        in_specs=[whole(pltpu.SMEM)] + [whole()] * (zone_count + 5),
        out_specs=[whole()] * 3,
        scratch_shapes=[pltpu.VMEM((RIM + length, columns), BF16)],
        compiler_params=params(),
        cost_estimate=cost(20 * length * columns, 4 * length * columns, length * columns),
    )(me, own, *zones, side, others, rim, weight, bias)


def block_state(b_block, x_ref, q_block, expand_ref, columns):
    weight = jnp.dot(q_block, expand_ref[:, columns], preferred_element_type=F32)
    scaled = (x_ref[:, columns].astype(F32) * weight).astype(BF16)
    return lax.dot_general(
        b_block, scaled, (((0,), (0,)), ((), ())), preferred_element_type=F32
    )


def tiles(width):
    step = min(512, width)
    return [slice(i, i + step) for i in range(0, width, step)]


def later_states_kernel(b_ref, x_ref, q_ref, dec_ref, starts_ref, total_ref, expand_ref):
    step = pl.program_id(0)

    @pl.when(step == 0)
    def _():
        expander(expand_ref, 1)
        total_ref[...] = jnp.zeros_like(total_ref)

    b_block = b_ref[...]
    q_block = q_ref[...].astype(BF16)
    for columns in tiles(x_ref.shape[1]):
        before = total_ref[:, columns]
        starts_ref[0, :, columns] = before.astype(BF16)
        decay = dec_ref[pl.ds(step + 1, 1), columns]
        total_ref[:, columns] = decay * before + block_state(
            b_block, x_ref, q_block, expand_ref, columns
        )


def later_states(b_act, x, q, dec):
    length, width = x.shape
    count = length // BLOCK - 1
    return pl.pallas_call(
        later_states_kernel,
        grid=(count,),
        out_shape=[
            jax.ShapeDtypeStruct((count, STATE, width), BF16),
            jax.ShapeDtypeStruct((STATE, width), F32),
        ],
        in_specs=[
            pl.BlockSpec((BLOCK, STATE), lambda c: (c + 1, 0)),
            pl.BlockSpec((BLOCK, width), lambda c: (c + 1, 0)),
            pl.BlockSpec((BLOCK, 128), lambda c: (c + 1, 0)),
            pl.BlockSpec(dec.shape, lambda c: (0, 0)),
        ],
        out_specs=[
            pl.BlockSpec((1, STATE, width), lambda c: (c, 0, 0)),
            pl.BlockSpec((STATE, width), lambda c: (0, 0)),
        ],
        scratch_shapes=[pltpu.VMEM((128, width), BF16)],
        compiler_params=params(),
        cost_estimate=cost(4 * length * STATE * width, 4 * length * width),
    )(b_act, x, q, dec)


def first_state_kernel(
    b_ref, first_ref, rim_ref, weight_ref, bias_ref, x_ref, q_ref, dec_ref, later_ref,
    b_out, state_ref, total_ref, expand_ref,
):
    expander(expand_ref, 1)
    slab = jnp.concatenate([rim_ref[...], first_ref[...]], axis=0).astype(F32)
    fixed = conv_slab(slab, weight_ref[...], bias_ref[...])
    b_block = jnp.concatenate([fixed, b_ref[RIM:, :]], axis=0)
    b_out[...] = b_block
    q_block = q_ref[...].astype(BF16)
    row = dec_ref.shape[0] - 2
    for columns in tiles(x_ref.shape[1]):
        state = block_state(b_block, x_ref, q_block, expand_ref, columns)
        state_ref[:, columns] = state
        total = later_ref[:, columns] + dec_ref[row : row + 1, columns] * state
        total_ref[:, columns] = total.astype(BF16)


def first_state(b_act, first, rim, weight, bias, x, q, dec, later):
    length, width = x.shape
    full = lambda a: pl.BlockSpec(a.shape, lambda c: (0,) * a.ndim)
    return pl.pallas_call(
        first_state_kernel,
        grid=(1,),
        out_shape=[
            jax.ShapeDtypeStruct(b_act.shape, BF16),
            jax.ShapeDtypeStruct((STATE, width), F32),
            jax.ShapeDtypeStruct((STATE, width), BF16),
        ],
        in_specs=[
            pl.BlockSpec((BLOCK, STATE), lambda c: (0, 0)),
            full(first), full(rim), full(weight), full(bias),
            pl.BlockSpec((BLOCK, width), lambda c: (0, 0)),
            pl.BlockSpec((BLOCK, 128), lambda c: (0, 0)),
            full(dec), full(later),
        ],
        out_specs=[
            pl.BlockSpec((BLOCK, STATE), lambda c: (0, 0)),
            pl.BlockSpec((STATE, width), lambda c: (0, 0)),
            pl.BlockSpec((STATE, width), lambda c: (0, 0)),
        ],
        scratch_shapes=[pltpu.VMEM((128, width), BF16)],
        input_output_aliases={0: 0},
        compiler_params=params(),
        cost_estimate=cost(4 * BLOCK * STATE * width, 12 * BLOCK * width),
    )(b_act, first, rim, weight, bias, x, q, dec, later)


def inner_kernel(
    c_ref, b_ref, x_ref, q_ref, brow_ref, starts_ref, state_ref, dec_ref, skip_ref,
    out_ref, expand_ref,
):
    step = pl.program_id(0)
    block_count = pl.num_programs(0)
    half = BLOCK // 2

    @pl.when(step == 0)
    def _():
        expander(expand_ref, 3)

    c_block = c_ref[...]
    gram = lax.dot_general(
        c_block, b_ref[...], (((1,), (1,)), ((), ())), preferred_element_type=F32
    )
    lower = lax.broadcasted_iota(jnp.int32, (half, half), 0) >= lax.broadcasted_iota(
        jnp.int32, (half, half), 1
    )
    gram_00 = jnp.where(lower, gram[:half, :half], 0.0)
    gram_10 = gram[half:, :half]
    gram_11 = jnp.where(lower, gram[half:, half:], 0.0)
    q_block = q_ref[...]
    q_short = q_block.astype(BF16)
    head_count = x_ref.shape[1] // HEAD_DIM
    for h in range(head_count):
        columns = slice(h * HEAD_DIM, (h + 1) * HEAD_DIM)
        rise = jnp.broadcast_to(q_block[:, h : h + 1], (BLOCK, half))
        fall = brow_ref[h : h + 1, :]
        w_00 = gram_00 * jnp.exp2(jnp.minimum(rise[:half] - fall[:, :half], 120.0))
        w_10 = gram_10 * jnp.exp2(rise[half:] - fall[:, :half])
        w_11 = gram_11 * jnp.exp2(jnp.minimum(rise[half:] - fall[:, half:], 120.0))
        x_head = x_ref[:, columns]
        top = jnp.dot(w_00.astype(BF16), x_head[:half], preferred_element_type=F32)
        low = jnp.concatenate([w_10.astype(BF16), w_11.astype(BF16)], axis=1)
        bottom = jnp.dot(low, x_head, preferred_element_type=F32)
        out_ref[:, columns] = jnp.concatenate([top, bottom], axis=0) + skip_ref[
            :, columns
        ] * x_head.astype(F32)

    @pl.when(step > 0)
    def _():
        for columns in tiles(x_ref.shape[1]):
            decay = dec_ref[pl.ds(block_count + step, 1), columns]
            start = starts_ref[0, :, columns].astype(F32) + decay * state_ref[:, columns]
            grown = jnp.dot(q_short, expand_ref[:, columns], preferred_element_type=F32)
            carried = jnp.dot(c_block, start.astype(BF16), preferred_element_type=F32)
            out_ref[:, columns] += grown * carried


def inner(c_act, b_act, x, q, brow, starts, state, dec, skip):
    length, width = x.shape
    count = length // BLOCK
    full = lambda a: pl.BlockSpec(a.shape, lambda c: (0,) * a.ndim)
    return pl.pallas_call(
        inner_kernel,
        grid=(count,),
        out_shape=jax.ShapeDtypeStruct((length, width), F32),
        in_specs=[
            pl.BlockSpec((BLOCK, STATE), lambda c: (c, 0)),
            pl.BlockSpec((BLOCK, STATE), lambda c: (c, 0)),
            pl.BlockSpec((BLOCK, width), lambda c: (c, 0)),
            pl.BlockSpec((BLOCK, 128), lambda c: (c, 0)),
            pl.BlockSpec((SLOT, BLOCK), lambda c: (0, c)),
            pl.BlockSpec((1, STATE, width), lambda c: (jnp.maximum(c - 1, 0), 0, 0)),
            full(state), full(dec), full(skip),
        ],
        out_specs=pl.BlockSpec((BLOCK, width), lambda c: (c, 0)),
        scratch_shapes=[pltpu.VMEM((128, width), BF16)],
        compiler_params=params(),
        cost_estimate=cost(8 * length * STATE * width, 8 * length * width, length * width * 2),
    )(c_act, b_act, x, q, brow, starts, state, dec, skip)


def gate_kernel(c_ref, y_ref, z_ref, q_ref, in_ref, out_ref, sum_ref, expand_ref):
    @pl.when(pl.program_id(0) == 0)
    def _():
        expander(expand_ref, 5)

    c_block = c_ref[...]
    q_short = q_ref[...].astype(BF16)
    squares = jnp.zeros((BLOCK, 128), F32)
    for columns in tiles(y_ref.shape[1]):
        grown = jnp.dot(q_short, expand_ref[:, columns], preferred_element_type=F32)
        carried = jnp.dot(c_block, in_ref[:, columns], preferred_element_type=F32)
        gated = (y_ref[:, columns] + grown * carried) * silu(z_ref[:, columns].astype(F32))
        out_ref[:, columns] = gated
        square = gated * gated
        for i in range(0, square.shape[1], 128):
            squares = squares + square[:, i : i + 128]
    sum_ref[...] = lax.dot_general(
        jnp.ones((8, 128), F32), squares, (((1,), (1,)), ((), ())),
        precision=HIGHEST, preferred_element_type=F32,
    )[0:1]


def gate(c_act, y, z, q, incoming):
    length, width = y.shape
    count = length // BLOCK
    return pl.pallas_call(
        gate_kernel,
        grid=(count,),
        out_shape=[
            jax.ShapeDtypeStruct((length, width), F32),
            jax.ShapeDtypeStruct((1, length), F32),
        ],
        in_specs=[
            pl.BlockSpec((BLOCK, STATE), lambda c: (c, 0)),
            pl.BlockSpec((BLOCK, width), lambda c: (c, 0)),
            pl.BlockSpec((BLOCK, width), lambda c: (c, 0)),
            pl.BlockSpec((BLOCK, 128), lambda c: (c, 0)),
            pl.BlockSpec((STATE, width), lambda c: (0, 0)),
        ],
        out_specs=[
            pl.BlockSpec((BLOCK, width), lambda c: (c, 0)),
            pl.BlockSpec((1, BLOCK), lambda c: (0, c)),
        ],
        scratch_shapes=[pltpu.VMEM((128, width), BF16)],
        input_output_aliases={1: 0},
        compiler_params=params(),
        cost_estimate=cost(4 * length * STATE * width, 10 * length * width, length * width),
    )(c_act, y, z, q, incoming)


def norm_kernel(g_ref, one_ref, two_ref, gain_ref, out_ref):
    square_sum = one_ref[...] + two_ref[...]
    inverse = lax.rsqrt(square_sum / INNER + 1e-05)
    scale = jnp.broadcast_to(inverse, (128, BLOCK)).T
    for i in range(0, g_ref.shape[1], 128):
        columns = slice(i, i + 128)
        out_ref[:, columns] = (g_ref[:, columns] * scale * gain_ref[:, columns]).astype(BF16)


def norm(gated, one, two, gain):
    length, width = gated.shape
    return pl.pallas_call(
        norm_kernel,
        grid=(length // BLOCK,),
        out_shape=jax.ShapeDtypeStruct((length, width), BF16),
        in_specs=[
            pl.BlockSpec((BLOCK, width), lambda c: (c, 0)),
            pl.BlockSpec((1, BLOCK), lambda c: (0, c)),
            pl.BlockSpec((1, BLOCK), lambda c: (0, c)),
            pl.BlockSpec((1, width), lambda c: (0, 0)),
        ],
        out_specs=pl.BlockSpec((BLOCK, width), lambda c: (c, 0)),
        compiler_params=params(),
        cost_estimate=cost(4 * length * width, 6 * length * width),
    )(gated, one, two, gain)


def zone_shift(a, k):
    size = lax.axis_size("head")
    return lax.ppermute(a, "head", [(i, (i + 2 * k) % size) for i in range(size)])


def side_swap(a):
    size = lax.axis_size("head")
    return lax.ppermute(a, "head", [(i, i ^ 1) for i in range(size)])


def gather(own):
    zone_count = lax.axis_size("head") // 2
    zones = [zone_shift(own, k) for k in range(1, zone_count)]
    side = side_swap(own)
    others = side_swap(jnp.concatenate(zones, axis=0))
    return own, zones, side, others


def spread_heads(rows):
    return jnp.repeat(rows, HEAD_DIM, axis=1)


def chained_state(total, log_total):
    size = lax.axis_size("seq")
    place = lax.axis_index("seq")
    if size == 4:
        swap = [(0, 1), (1, 0), (2, 3), (3, 2)]
        odd = lax.rem(place, 2) == 1
        half = total.shape[1] // 2
        partner_log = lax.ppermute(log_total, "seq", swap)
        own_decay = spread_heads(jnp.exp(log_total)[None, :])
        partner_decay = spread_heads(jnp.exp(partner_log)[None, :])
        early, late = total[:, :half], total[:, half:]
        kept = jnp.where(odd, early, late)
        got = lax.ppermute(jnp.where(odd, late, early), "seq", swap)
        kept_partner_decay = jnp.where(odd, partner_decay[:, :half], partner_decay[:, half:])
        kept_own_decay = jnp.where(odd, own_decay[:, :half], own_decay[:, half:])
        kept_f, got_f = kept.astype(F32), got.astype(F32)
        both = jnp.where(
            odd, kept_own_decay * got_f + kept_f, kept_partner_decay * kept_f + got_f
        )
        crossed = lax.ppermute(both.astype(BF16), "seq", [(0, 2), (1, 3)])
        crossed_f = crossed.astype(F32)
        after_even = (
            jnp.where(odd, kept_partner_decay, kept_own_decay) * crossed_f
            + jnp.where(odd, got_f, kept_f)
        ).astype(BF16)
        last = lax.ppermute(jnp.where(odd, crossed, after_even), "seq", swap)
        return jnp.concatenate(
            [jnp.where(odd, after_even, last), jnp.where(odd, last, crossed)], axis=1
        )
    totals = lax.all_gather(total, "seq")
    logs = lax.all_gather(log_total, "seq")

    def one(hop, state):
        decay = spread_heads(jnp.exp(lax.dynamic_index_in_dim(logs, hop, 0, True)))
        return decay * state + lax.dynamic_index_in_dim(totals, hop, 0, False).astype(F32)

    return lax.fori_loop(0, place, one, jnp.zeros(total.shape, F32)).astype(BF16)


def on_device(x_inner, z_gate, bc_raw, conv_weight, conv_bias, dt_raw, a_log, d_skip, norm_gain):
    length = x_inner.shape[0]
    head_count = a_log.shape[0]
    block_count = length // BLOCK
    own_rows = bc_raw.shape[0]
    seq_size = lax.axis_size("seq")
    me = lax.axis_index("head").astype(jnp.int32).reshape(1)
    weight_b, weight_c = conv_weight[:, :STATE], conv_weight[:, STATE:]
    bias_b, bias_c = conv_bias[None, :STATE], conv_bias[None, STATE:]
    no_rim = jnp.zeros((RIM, STATE), BF16)

    own_c = bc_raw[:, STATE:]
    own_b = jnp.concatenate([bc_raw[:, :STATE], own_c[-RIM:]], axis=0)
    parts_b = gather(own_b)
    parts_c = gather(own_c)

    pad = ((0, SLOT - head_count), (0, 0))
    q, brow, ends = rates(jnp.pad(dt_raw.T, pad), jnp.pad(a_log[:, None], pad))
    end = ends[:head_count, :block_count].T
    log_total = jnp.sum(end, axis=0)
    from_one = jnp.cumsum(end[1:], axis=0)
    nothing = jnp.zeros((2, head_count), F32)
    logs = jnp.concatenate([end, nothing, from_one, log_total[None]], axis=0)
    dec = spread_heads(jnp.exp(logs))
    skip = spread_heads(d_skip[None, :])

    b_act, first_b, last_rows = activate(me, *parts_b, no_rim, weight_b, bias_b, own_rows)
    rims = lax.ppermute(last_rows, "seq", [(i, i + 1) for i in range(seq_size - 1)])
    starts, later = later_states(b_act, x_inner, q, dec)
    b_act, state_0, total = first_state(
        b_act, first_b, rims[:RIM], weight_b, bias_b, x_inner, q, dec, later
    )
    incoming = chained_state(total, log_total)
    c_act, _, _ = activate(me, *parts_c, rims[RIM:], weight_c, bias_c, own_rows)
    local = inner(c_act, b_act, x_inner, q, brow, starts, state_0, dec, skip)
    gated, squares = gate(c_act, local, z_gate, q, incoming)
    for k in range(1, lax.axis_size("head") // 2):
        squares = squares if k > 1 else [squares]
        squares.append(zone_shift(squares[0], k))
    column = sum(squares[1:], squares[0])
    return norm(gated, column, side_swap(column), norm_gain[None, :])


def solution(mesh):
    placed = (
        P("seq", "head"),
        P("seq", "head"),
        P(("seq", "head"), None),
        P(),
        P(),
        P("seq", "head"),
        P("head"),
        P("head"),
        P("head"),
    )
    return jax.shard_map(
        on_device, mesh=mesh, in_specs=placed, out_specs=P("seq", "head"), check_vma=False
    )
```

```python
import functools
import math

import jax
import jax.numpy as jnp
from jax import lax
from jax.experimental import pallas as pl
from jax.experimental.pallas import tpu as pltpu
from jax.sharding import PartitionSpec as P

HEAD_DIM = 128
STATE = 256
BLOCK = 256
INNER = 16384
RIM = 16
SLOT = 16
LOG2E = math.log2(math.e)
F32 = jnp.float32
BF16 = jnp.bfloat16
HIGHEST = lax.Precision.HIGHEST
VMEM_LIMIT = 14 * 1024 * 1024


def params():
    return pltpu.CompilerParams(vmem_limit_bytes=VMEM_LIMIT)


def whole(memory_space=pltpu.VMEM):
    return pl.BlockSpec(memory_space=memory_space)


def kept_in_vmem(shape, dtype):
    return pltpu.VMEM(shape, dtype)


def stream_in(hbm_ref, held, sems, columns=None):
    copies = []
    for c in range(held.shape[0]):
        rows = pl.ds(c * BLOCK, BLOCK)
        source = hbm_ref.at[rows, :] if columns is None else hbm_ref.at[rows, columns]
        copy = pltpu.make_async_copy(source, held.at[c], sems.at[c])
        copy.start()
        copies.append(copy)
    return copies


def in_hbm(a):
    return pltpu.with_memory_space_constraint(a, pltpu.HBM)


def cost(flops, nbytes, trans=0):
    return pl.CostEstimate(flops=int(flops), bytes_accessed=int(nbytes), transcendentals=int(trans))


def silu(v):
    half = 0.5 * v
    return half + half * jnp.tanh(half)


def split(v):
    high = v.astype(BF16).astype(F32)
    return high, v - high


def conv_slab(slab, weight, bias):
    taps = weight.shape[0]
    total = jnp.broadcast_to(bias, slab.shape)
    for k in range(taps):
        shift = taps - 1 - k
        moved = pltpu.roll(slab, shift, 0) if shift else slab
        total = total + weight[k : k + 1, :] * moved
    total = total[RIM:]
    return (total * jax.nn.sigmoid(total)).astype(BF16)


def rates_kernel(dt_ref, a_ref, skip_ref, q_ref, b_ref, dec_ref, own_ref):
    block_count = dt_ref.shape[1] // BLOCK
    diagonal = lax.broadcasted_iota(jnp.int32, (SLOT, SLOT), 0) == lax.broadcasted_iota(
        jnp.int32, (SLOT, SLOT), 1
    )

    def upright(row):
        return jnp.sum(jnp.where(diagonal, row, 0.0), axis=1, keepdims=True)

    rate = -jnp.exp(upright(a_ref[...]))
    upper = (
        lax.broadcasted_iota(jnp.int32, (BLOCK, BLOCK), 0)
        <= lax.broadcasted_iota(jnp.int32, (BLOCK, BLOCK), 1)
    ).astype(F32)
    prior = jnp.zeros((SLOT, 1), F32)
    later = jnp.zeros((SLOT, 1), F32)
    lane = lax.broadcasted_iota(jnp.int32, (SLOT, SLOT), 1)
    logs = jnp.zeros((SLOT, SLOT), F32)
    for c in range(block_count):
        columns = slice(c * BLOCK, (c + 1) * BLOCK)
        dt = dt_ref[:, columns]
        step = jnp.maximum(dt, 0.0) + jnp.log1p(jnp.exp(-jnp.abs(dt)))
        cum = jnp.dot(rate * step, upper, precision=HIGHEST, preferred_element_type=F32)
        last = cum[:, BLOCK - 1 : BLOCK]
        scaled = cum * LOG2E
        b_ref[:, columns] = scaled - jnp.log(step) * LOG2E
        parts = [scaled]
        parts.extend(split(jnp.exp(last - cum) * step))
        parts.extend(split(jnp.exp(cum)))
        parts.extend(split(jnp.exp(cum + prior)))
        parts.append(jnp.zeros_like(cum))
        q_ref[columns, :] = jnp.concatenate(parts, axis=0).T
        logs = jnp.where(lane == c, last, logs)
        logs = jnp.where(lane == block_count + c, later, logs)
        prior = prior + last
        if c > 0:
            later = later + last
    logs = jnp.where(lane == 2 * block_count, later, logs)
    logs = jnp.where(lane == SLOT - 1, prior, logs)
    factors = jnp.where(lane == 2 * block_count + 1, upright(skip_ref[...]), jnp.exp(logs))
    width = dec_ref.shape[1]
    head = lax.broadcasted_iota(jnp.int32, (SLOT, width), 1) // HEAD_DIM
    spread = (lax.broadcasted_iota(jnp.int32, (SLOT, width), 0) == head).astype(F32)
    rows = lax.dot_general(
        factors, spread, (((0,), (0,)), ((), ())), precision=HIGHEST, preferred_element_type=F32
    )
    dec_ref[...] = rows
    own_ref[...] = rows[SLOT - 1 : SLOT]


def rates(dt, a_log, d_skip, width):
    length = dt.shape[1]
    return pl.pallas_call(
        rates_kernel,
        out_shape=[
            kept_in_vmem((length, 128), F32),
            kept_in_vmem((SLOT, length), F32),
            kept_in_vmem((SLOT, width), F32),
            kept_in_vmem((1, width), F32),
        ],
        in_specs=[whole()] * 3,
        out_specs=[whole()] * 4,
        compiler_params=params(),
        cost_estimate=cost(0, 0),
    )(dt, a_log, d_skip)


def expander(ref, slot, base):
    row = lax.broadcasted_iota(jnp.int32, ref.shape, 0)
    head = (lax.broadcasted_iota(jnp.int32, ref.shape, 1) + base) // HEAD_DIM
    ref[...] = ((row == slot * SLOT + head) | (row == (slot + 1) * SLOT + head)).astype(BF16)


def prepare_kernel(place_ref, bc_ref, b_ref, c_ref, place_out):
    rows = bc_ref.shape[0]
    for i in range(place_ref.shape[0]):
        place_out[i] = place_ref[i]
    b_ref[0:rows, :] = bc_ref[:, :STATE]
    b_ref[rows : rows + RIM, :] = bc_ref[rows - RIM :, STATE:]
    c_ref[...] = bc_ref[:, STATE:]


def prepare(place, bc_raw):
    rows = bc_raw.shape[0]
    return pl.pallas_call(
        prepare_kernel,
        out_shape=[
            jax.ShapeDtypeStruct((rows + RIM, STATE), BF16),
            jax.ShapeDtypeStruct((rows, STATE), BF16),
            pltpu.SMEM(place.shape, jnp.int32),
        ],
        in_specs=[whole(pltpu.SMEM), whole()],
        out_specs=[whole(), whole(), whole(pltpu.SMEM)],
        compiler_params=params(),
        cost_estimate=cost(0, 0),
    )(place, bc_raw)


def pack_kernel(*refs):
    own_ref, side_ref, _, cat_ref, pair_ref = refs[-5:]
    per = refs[0].shape[0]
    for i, ref in enumerate(refs[:-5]):
        cat_ref[i * per : (i + 1) * per, :] = ref[...]
    rows = own_ref.shape[0]
    pair_ref[0:rows, :] = own_ref[...]
    pair_ref[rows : 2 * rows, :] = side_ref[...]


def pack(zones, own, side, after):
    rows, columns = zones[0].shape
    return pl.pallas_call(
        pack_kernel,
        out_shape=[
            jax.ShapeDtypeStruct((len(zones) * rows, columns), BF16),
            jax.ShapeDtypeStruct((2 * own.shape[0], columns), BF16),
        ],
        in_specs=[whole()] * (len(zones) + 2) + [whole(pl.ANY)],
        out_specs=[whole()] * 2,
        compiler_params=params(),
        cost_estimate=cost(0, 0),
    )(*zones, own, side, after)


def act_kernel(own_rows, plan, is_b, me_ref, weight_ref, bias_ref, *refs):
    sources = refs[: 1 + max(index for index, *_ in plan) + (not is_b)]
    act_ref, first_ref, last_ref, raw = refs[-4:]
    me = me_ref[0]
    size = act_ref.shape[0] // own_rows
    partner = me + 1 - 2 * lax.rem(me, 2)
    if is_b:
        raw[0:RIM, :] = jnp.zeros((RIM, STATE), BF16)
    else:
        raw[0:RIM, :] = sources[-1][RIM : 2 * RIM, :]
    for index, start, side, shift in plan:
        ref = sources[index]
        owner = lax.rem((partner if side else me) - 2 * shift + size, size)
        at = pl.multiple_of(RIM + owner * own_rows, 16)
        raw[pl.ds(at, own_rows), :] = ref[start : start + own_rows, :]
        if is_b:

            @pl.when(owner == size - 1)
            def _(ref=ref, start=start):
                end = start + own_rows
                last_ref[0:RIM, :] = ref[end - RIM : end, :]
                last_ref[RIM : 2 * RIM, :] = ref[end : end + RIM, :]

    first_ref[...] = raw[RIM : 2 * RIM, :]
    part = slice(0, STATE) if is_b else slice(STATE, 2 * STATE)
    weight = weight_ref[:, part]
    bias = bias_ref[:, part]
    for c in range(act_ref.shape[0] // BLOCK):
        slab = raw[c * BLOCK : c * BLOCK + RIM + BLOCK, :].astype(F32)
        act_ref[c * BLOCK : (c + 1) * BLOCK, :] = conv_slab(slab, weight, bias)


def activate(me, sources, plan, is_b, weight, bias, own_rows, after=()):
    length = len(plan) * own_rows
    return pl.pallas_call(
        functools.partial(act_kernel, own_rows, plan, is_b),
        out_shape=[
            kept_in_vmem((length, STATE), BF16),
            kept_in_vmem((RIM, STATE), BF16),
            kept_in_vmem((2 * RIM, STATE), BF16),
        ],
        in_specs=[whole(pltpu.SMEM)]
        + [whole()] * (len(sources) + 2)
        + [whole(pl.ANY)] * len(after),
        out_specs=[whole()] * 3,
        scratch_shapes=[pltpu.VMEM((RIM + length, STATE), BF16)],
        compiler_params=params(),
        cost_estimate=cost(0, 0),
    )(me, weight, bias, *sources, *after)


def tiles(width):
    step = min(512, width)
    return [slice(i, i + step) for i in range(0, width, step)]


def scale_kernel(x_ref, q_ref, first_ref, later_ref, expand_ref, held, sems):
    copies = stream_in(x_ref, held, sems)
    expander(expand_ref, 1, 0)
    for c, copy in enumerate(copies):
        rows = slice(c * BLOCK, (c + 1) * BLOCK)
        q_block = q_ref[rows, :].astype(BF16)
        copy.wait()
        for columns in tiles(x_ref.shape[1]):
            weight = jnp.dot(q_block, expand_ref[:, columns], preferred_element_type=F32)
            scaled = (held[c, :, columns].astype(F32) * weight).astype(BF16)
            if c == 0:
                first_ref[:, columns] = scaled
            else:
                later_ref[(c - 1) * BLOCK : c * BLOCK, columns] = scaled


def scale(x, q):
    length, width = x.shape
    count = length // BLOCK
    return pl.pallas_call(
        scale_kernel,
        out_shape=[
            kept_in_vmem((BLOCK, width), BF16),
            kept_in_vmem((length - BLOCK, width), BF16),
        ],
        in_specs=[whole(pltpu.HBM), whole()],
        out_specs=[whole()] * 2,
        scratch_shapes=[
            pltpu.VMEM((128, width), BF16),
            pltpu.VMEM((count, BLOCK, width), BF16),
            pltpu.SemaphoreType.DMA((count,)),
        ],
        compiler_params=params(),
        cost_estimate=cost(0, 0),
    )(x, q)


def block_state(b_block, scaled):
    return lax.dot_general(
        b_block, scaled, (((0,), (0,)), ((), ())), preferred_element_type=F32
    )


def later_states_kernel(b_ref, xs_ref, dec_ref, *refs):
    starts_ref, total_ref = refs[-2:]
    for c in range(1, b_ref.shape[0] // BLOCK):
        rows = slice(c * BLOCK, (c + 1) * BLOCK)
        b_block = b_ref[rows, :]
        for columns in tiles(xs_ref.shape[1]):
            state = block_state(b_block, xs_ref[(c - 1) * BLOCK : c * BLOCK, columns])
            if c == 1:
                starts_ref[0, :, columns] = jnp.zeros_like(state).astype(BF16)
                total_ref[:, columns] = state
            else:
                before = total_ref[:, columns]
                starts_ref[c - 1, :, columns] = before.astype(BF16)
                total_ref[:, columns] = dec_ref[c : c + 1, columns] * before + state


def later_states(b_act, xs, dec, after=()):
    length, width = xs.shape
    return pl.pallas_call(
        later_states_kernel,
        out_shape=[
            kept_in_vmem((length // BLOCK, STATE, width), BF16),
            kept_in_vmem((STATE, width), F32),
        ],
        in_specs=[whole()] * 3 + [whole(pl.ANY)] * len(after),
        out_specs=[whole()] * 2,
        compiler_params=params(),
        cost_estimate=cost(0, 0),
    )(b_act, xs, dec, *after)


def first_state_kernel(
    at_ref, b_ref, first_ref, rim_ref, weight_ref, bias_ref, xs_ref, dec_ref, later_ref, *refs
):
    b_out, state_ref, kept_ref, sent_ref, total_ref = refs[-5:]
    slab = jnp.concatenate([rim_ref[0:RIM, :], first_ref[...]], axis=0).astype(F32)
    fixed = conv_slab(slab, weight_ref[:, :STATE], bias_ref[:, :STATE])
    b_block = jnp.concatenate([fixed, b_ref[RIM:BLOCK, :]], axis=0)
    b_out[0:RIM, :] = fixed
    row = 2 * (b_out.shape[0] // BLOCK)
    for columns in tiles(xs_ref.shape[1]):
        state = block_state(b_block, xs_ref[0:BLOCK, columns])
        state_ref[:, columns] = state
        total = later_ref[:, columns] + dec_ref[row : row + 1, columns] * state
        total_ref[:, columns] = total.astype(BF16)
    half = kept_ref.shape[1]
    at = pl.multiple_of(at_ref[1], 128)
    kept_ref[...] = total_ref[:, pl.ds(at, half)]
    sent_ref[...] = total_ref[:, pl.ds(pl.multiple_of(half - at, 128), half)]


def first_state(at, b_act, first, rim, weight, bias, xs, dec, later, after=()):
    width = xs.shape[1]
    return pl.pallas_call(
        first_state_kernel,
        out_shape=[
            kept_in_vmem(b_act.shape, BF16),
            kept_in_vmem((STATE, width), F32),
            kept_in_vmem((STATE, width // 2), BF16),
            kept_in_vmem((STATE, width // 2), BF16),
        ],
        in_specs=[whole(pltpu.SMEM)] + [whole()] * 8 + [whole(pl.ANY)] * len(after),
        out_specs=[whole()] * 4,
        scratch_shapes=[pltpu.VMEM((STATE, width), BF16)],
        input_output_aliases={1: 0},
        compiler_params=params(),
        cost_estimate=cost(0, 0),
    )(at, b_act, first, rim, weight, bias, xs, dec, later, *after)


def meet_kernel(at_ref, kept_ref, got_ref, own_ref, partner_ref, out_ref):
    half = kept_ref.shape[1]
    columns = pl.ds(pl.multiple_of(at_ref[1], 128), half)
    odd = at_ref[1] == 0
    kept_decay = jnp.where(odd, 1.0, partner_ref[:, columns])
    got_decay = jnp.where(odd, own_ref[:, columns], 1.0)
    both = kept_decay * kept_ref[...].astype(F32) + got_decay * got_ref[...].astype(F32)
    out_ref[...] = both.astype(BF16)


def meet(at, kept, got, own, partner):
    return pl.pallas_call(
        meet_kernel,
        out_shape=kept_in_vmem(kept.shape, BF16),
        in_specs=[whole(pltpu.SMEM)] + [whole()] * 4,
        out_specs=whole(),
        compiler_params=params(),
        cost_estimate=cost(0, 0),
    )(at, kept, got, own, partner)


def arrive_kernel(at_ref, crossed_ref, kept_ref, got_ref, own_ref, partner_ref, *refs):
    in_ref, sent_ref = refs[-2:]
    half = kept_ref.shape[1]
    columns = pl.ds(pl.multiple_of(at_ref[1], 128), half)
    odd = at_ref[1] == 0
    decay = jnp.where(odd, partner_ref[:, columns], own_ref[:, columns])
    crossed = crossed_ref[...]
    mine = jnp.where(odd, got_ref[...].astype(F32), kept_ref[...].astype(F32))
    after_even = (decay * crossed.astype(F32) + mine).astype(BF16)
    in_ref[...] = jnp.where(odd, after_even, crossed)
    sent_ref[...] = jnp.where(odd, crossed, after_even)


def arrive(at, crossed, kept, got, own, partner, after):
    return pl.pallas_call(
        arrive_kernel,
        out_shape=[kept_in_vmem(kept.shape, BF16)] * 2,
        in_specs=[whole(pltpu.SMEM)] + [whole()] * 5 + [whole(pl.ANY)],
        out_specs=[whole()] * 2,
        compiler_params=params(),
        cost_estimate=cost(0, 0),
    )(at, crossed, kept, got, own, partner, after)


def inner_kernel(
    c_ref, b_ref, x_ref, q_ref, brow_ref, starts_ref, state_ref, dec_ref,
    out_ref, expand_ref, held, sems,
):
    stream_in(x_ref, held, sems)
    half = BLOCK // 2
    block_count = x_ref.shape[0] // BLOCK
    head_count = x_ref.shape[1] // HEAD_DIM
    expander(expand_ref, 3, 0)
    lower = lax.broadcasted_iota(jnp.int32, (half, half), 0) >= lax.broadcasted_iota(
        jnp.int32, (half, half), 1
    )

    @pl.loop(0, block_count)
    def _(c):
        at = pl.multiple_of(c * BLOCK, BLOCK)
        rows = pl.ds(at, BLOCK)
        pltpu.make_async_copy(x_ref.at[rows, :], held.at[c], sems.at[c]).wait()
        c_block = c_ref[rows, :]
        gram = lax.dot_general(
            c_block, b_ref[rows, :], (((1,), (1,)), ((), ())), preferred_element_type=F32
        )
        gram_00 = jnp.where(lower, gram[:half, :half], 0.0)
        gram_10 = gram[half:, :half]
        gram_11 = jnp.where(lower, gram[half:, half:], 0.0)
        q_block = q_ref[rows, :]
        q_short = q_block.astype(BF16)
        for h in range(head_count):
            columns = slice(h * HEAD_DIM, (h + 1) * HEAD_DIM)
            rise = jnp.broadcast_to(q_block[:, h : h + 1], (BLOCK, half))
            fall = brow_ref[h : h + 1, rows]
            w_00 = gram_00 * jnp.exp2(jnp.minimum(rise[:half] - fall[:, :half], 120.0))
            w_10 = gram_10 * jnp.exp2(rise[half:] - fall[:, :half])
            w_11 = gram_11 * jnp.exp2(jnp.minimum(rise[half:] - fall[:, half:], 120.0))
            x_head = held[c, :, columns]
            top = jnp.dot(w_00.astype(BF16), x_head[:half], preferred_element_type=F32)
            low = jnp.concatenate([w_10.astype(BF16), w_11.astype(BF16)], axis=1)
            bottom = jnp.dot(low, x_head, preferred_element_type=F32)
            out_ref[rows, columns] = jnp.concatenate([top, bottom], axis=0) + dec_ref[
                2 * block_count + 1 : 2 * block_count + 2, columns
            ] * x_head.astype(F32)

        @pl.when(c > 0)
        def _():
            for columns in tiles(x_ref.shape[1]):
                decay = dec_ref[pl.ds(block_count + c, 1), columns]
                start = starts_ref[c - 1, :, columns].astype(F32) + decay * state_ref[:, columns]
                grown = jnp.dot(q_short, expand_ref[:, columns], preferred_element_type=F32)
                carried = jnp.dot(c_block, start.astype(BF16), preferred_element_type=F32)
                out_ref[rows, columns] += grown * carried


def inner(c_act, b_act, x, q, brow, starts, state, dec):
    length, width = x.shape
    return pl.pallas_call(
        inner_kernel,
        out_shape=kept_in_vmem((length, width), F32),
        in_specs=[whole()] * 2 + [whole(pltpu.HBM)] + [whole()] * 5,
        out_specs=whole(),
        scratch_shapes=[
            pltpu.VMEM((128, width), BF16),
            pltpu.VMEM((length // BLOCK, BLOCK, width), BF16),
            pltpu.SemaphoreType.DMA((length // BLOCK,)),
        ],
        compiler_params=params(),
        cost_estimate=cost(0, 13 * length * width),
    )(c_act, b_act, x, q, brow, starts, state, dec)


def gate_kernel(second, at_ref, c_ref, y_ref, z_ref, q_ref, in_ref, *refs):
    out_ref, sum_ref, expand_ref, held, sems = refs[-5:]
    width = in_ref.shape[1]
    base = pl.multiple_of(width - at_ref[1] if second else at_ref[1], 128)
    stream_in(z_ref, held, sems, pl.ds(base, width))
    expander(expand_ref, 5, base)

    @pl.loop(0, y_ref.shape[0] // BLOCK)
    def _(c):
        rows = pl.ds(pl.multiple_of(c * BLOCK, BLOCK), BLOCK)
        pltpu.make_async_copy(z_ref.at[rows, pl.ds(base, width)], held.at[c], sems.at[c]).wait()
        c_block = c_ref[rows, :]
        q_short = q_ref[rows, :].astype(BF16)
        squares = jnp.zeros((BLOCK, 128), F32)
        for part in tiles(width):
            size = part.stop - part.start
            columns = pl.ds(pl.multiple_of(base + part.start, 128), size)
            grown = jnp.dot(q_short, expand_ref[:, part], preferred_element_type=F32)
            carried = jnp.dot(c_block, in_ref[:, part], preferred_element_type=F32)
            gated = (y_ref[rows, columns] + grown * carried) * silu(held[c, :, part].astype(F32))
            out_ref[rows, columns] = gated
            square = gated * gated
            for i in range(0, size, 128):
                squares = squares + square[:, i : i + 128]
        total = lax.dot_general(
            jnp.ones((8, 128), F32), squares, (((1,), (1,)), ((), ())),
            precision=HIGHEST, preferred_element_type=F32,
        )[0:1]
        sum_ref[:, rows] = refs[0][:, rows] + total if second else total


def gate(at, c_act, y, z, q, incoming, *before):
    length, width = y.shape
    return pl.pallas_call(
        functools.partial(gate_kernel, len(before) > 0),
        out_shape=[
            kept_in_vmem((length, width), F32),
            kept_in_vmem((1, length), F32),
        ],
        in_specs=[whole(pltpu.SMEM)]
        + [whole()] * 2
        + [whole(pltpu.HBM)]
        + [whole()] * (2 + len(before)),
        out_specs=[whole()] * 2,
        scratch_shapes=[
            pltpu.VMEM((128, incoming.shape[1]), BF16),
            pltpu.VMEM((length // BLOCK, BLOCK, incoming.shape[1]), BF16),
            pltpu.SemaphoreType.DMA((length // BLOCK,)),
        ],
        input_output_aliases={2: 0},
        compiler_params=params(),
        cost_estimate=cost(0, 8 * length * width),
    )(at, c_act, y, z, q, incoming, *before)


def norm_kernel(g_ref, one_ref, two_ref, gain_ref, out_ref, held, sems):
    copies = []
    for c in range(g_ref.shape[0] // BLOCK):
        rows = slice(c * BLOCK, (c + 1) * BLOCK)
        square_sum = one_ref[:, rows] + two_ref[:, rows]
        inverse = lax.rsqrt(square_sum / INNER + 1e-05)
        scale = jnp.broadcast_to(inverse, (128, BLOCK)).T
        for i in range(0, g_ref.shape[1], 128):
            columns = slice(i, i + 128)
            held[c, :, columns] = (g_ref[rows, columns] * scale * gain_ref[:, columns]).astype(BF16)
        copy = pltpu.make_async_copy(held.at[c], out_ref.at[rows, :], sems.at[c])
        copy.start()
        copies.append(copy)
    for copy in copies:
        copy.wait()


def norm(gated, one, two, gain):
    length, width = gated.shape
    count = length // BLOCK
    return pl.pallas_call(
        norm_kernel,
        out_shape=jax.ShapeDtypeStruct((length, width), BF16),
        in_specs=[whole()] * 4,
        out_specs=whole(pltpu.HBM),
        scratch_shapes=[
            pltpu.VMEM((count, BLOCK, width), BF16),
            pltpu.SemaphoreType.DMA((count,)),
        ],
        compiler_params=params(),
        cost_estimate=cost(0, 0),
    )(gated, one, two, gain)


SWAP = [(0, 1), (1, 0), (2, 3), (3, 2)]


def zone_shift(a, k):
    size = lax.axis_size("head")
    return lax.ppermute(a, "head", [(i, (i + 2 * k) % size) for i in range(size)])


def side_swap(a):
    size = lax.axis_size("head")
    return lax.ppermute(a, "head", [(i, i ^ 1) for i in range(size)])


def chained_state(at, kept, sent, own, partner, after):
    size = lax.axis_size("seq")
    if size == 4:
        got = lax.ppermute(sent, "seq", SWAP)
        both = meet(at, kept, got, own, partner)
        crossed = lax.ppermute(both, "seq", [(0, 2), (1, 3)])
        mine, passed = arrive(at, crossed, kept, got, own, partner, after)
        return mine, lax.ppermute(passed, "seq", SWAP)
    totals = lax.all_gather(jnp.concatenate([kept, sent], axis=1), "seq")
    decays = lax.all_gather(own, "seq")

    def one(hop, state):
        decay = lax.dynamic_index_in_dim(decays, hop, 0, False)
        return decay * state + lax.dynamic_index_in_dim(totals, hop, 0, False).astype(F32)

    place = lax.axis_index("seq")
    state = lax.fori_loop(0, place, one, jnp.zeros(totals.shape[1:], F32)).astype(BF16)
    half = kept.shape[1]
    return state[:, :half], state[:, half:]


def on_device(x_inner, z_gate, bc_raw, conv_weight, conv_bias, dt_raw, a_log, d_skip, norm_gain):
    x_inner, z_gate = in_hbm(x_inner), in_hbm(z_gate)
    head_count = a_log.shape[0]
    own_rows = bc_raw.shape[0]
    seq_size = lax.axis_size("seq")
    shifts = range(1, lax.axis_size("head") // 2)
    width = x_inner.shape[1]
    first_channel = 0
    if seq_size == 4:
        first_channel = (1 - lax.rem(lax.axis_index("seq"), 2)) * (width // 2)
    place = jnp.stack([lax.axis_index("head"), first_channel]).astype(jnp.int32)
    own_b, own_c, place = prepare(place, bc_raw)
    zones_b = [zone_shift(own_b, k) for k in shifts]
    side_b = side_swap(own_b)
    side_c = side_swap(own_c)
    pad = SLOT - head_count
    q, brow, dec, own_decay = rates(
        jnp.pad(dt_raw.T, ((0, pad), (0, 0))),
        jnp.pad(a_log, (0, pad))[None, :],
        jnp.pad(d_skip, (0, pad))[None, :],
        width,
    )
    cat_b, pair_c = pack(zones_b, own_c, side_c, own_decay)
    others_b = side_swap(cat_b)
    pairs_c = [zone_shift(pair_c, k) for k in shifts]
    sources_b = [own_b, side_b, *zones_b, others_b]
    plan_b = [(0, 0, False, 0), (1, 0, True, 0)]
    plan_b += [(k + 1, 0, False, k) for k in shifts]
    plan_b += [(len(zones_b) + 2, (k - 1) * own_b.shape[0], True, k) for k in shifts]
    sources_c = [pair_c, *pairs_c]
    plan_c = [(k, 0, False, k) for k in range(len(sources_c))]
    plan_c += [(k, own_rows, True, k) for k in range(len(sources_c))]

    bias = conv_bias[None, :]
    xs_first, xs_later = scale(x_inner, q)
    partner_decay = own_decay
    if seq_size == 4:
        partner_decay = lax.ppermute(own_decay, "seq", SWAP)
    b_act, first_b, last_rows = activate(
        place, sources_b, plan_b, True, conv_weight, bias, own_rows, [xs_first, pairs_c[0]]
    )
    rims = lax.ppermute(last_rows, "seq", [(i, i + 1) for i in range(seq_size - 1)])
    starts, later = later_states(b_act, xs_later, dec, [pairs_c[1]])
    b_act, state_0, kept, sent = first_state(
        place, b_act, first_b, rims, conv_weight, bias, xs_first, dec, later, [pairs_c[2]]
    )
    c_act, _, _ = activate(place, [*sources_c, rims], plan_c, False, conv_weight, bias, own_rows)
    local = inner(c_act, b_act, x_inner, q, brow, starts, state_0, dec)
    state_one, state_two = chained_state(place, kept, sent, own_decay, partner_decay, local)
    gated, square_one = gate(place, c_act, local, z_gate, q, state_one)
    gated, square_sum = gate(place, c_act, gated, z_gate, q, state_two, square_one)
    column = sum([zone_shift(square_sum, k) for k in shifts], square_sum)
    return norm(gated, column, side_swap(column), norm_gain[None, :])


def solution(mesh):
    placed = (
        P("seq", "head"),
        P("seq", "head"),
        P(("seq", "head"), None),
        P(),
        P(),
        P("seq", "head"),
        P("head"),
        P("head"),
        P("head"),
    )
    return jax.shard_map(
        on_device, mesh=mesh, in_specs=placed, out_specs=P("seq", "head"), check_vma=False
    )
```

```python
import functools
import math

import jax
import jax.numpy as jnp
from jax import lax
from jax.experimental import pallas as pl
from jax.experimental.pallas import tpu as pltpu
from jax.sharding import PartitionSpec as P

HEAD_DIM = 128
STATE = 256
BLOCK = 256
INNER = 16384
RIM = 16
SLOT = 16
LOG2E = math.log2(math.e)
F32 = jnp.float32
BF16 = jnp.bfloat16
HIGHEST = lax.Precision.HIGHEST
VMEM_LIMIT = 14 * 1024 * 1024


def params():
    return pltpu.CompilerParams(vmem_limit_bytes=VMEM_LIMIT)


def whole(memory_space=pltpu.VMEM):
    return pl.BlockSpec(memory_space=memory_space)


def kept_in_vmem(shape, dtype):
    return pltpu.VMEM(shape, dtype)


def stream_in(hbm_ref, held, sems, columns=None):
    copies = []
    for c in range(held.shape[0]):
        rows = pl.ds(c * BLOCK, BLOCK)
        source = hbm_ref.at[rows, :] if columns is None else hbm_ref.at[rows, columns]
        copy = pltpu.make_async_copy(source, held.at[c], sems.at[c])
        copy.start()
        copies.append(copy)
    return copies


def in_hbm(a):
    return pltpu.with_memory_space_constraint(a, pltpu.HBM)


def cost(flops, nbytes, trans=0):
    return pl.CostEstimate(flops=int(flops), bytes_accessed=int(nbytes), transcendentals=int(trans))


def silu(v):
    half = 0.5 * v
    return half + half * jnp.tanh(half)


def split(v):
    high = v.astype(BF16).astype(F32)
    return high, v - high


def conv_slab(slab, weight, bias):
    taps = weight.shape[0]
    total = jnp.broadcast_to(bias, slab.shape)
    for k in range(taps):
        shift = taps - 1 - k
        moved = pltpu.roll(slab, shift, 0) if shift else slab
        total = total + weight[k : k + 1, :] * moved
    total = total[RIM:]
    return (total * jax.nn.sigmoid(total)).astype(BF16)


def rates_kernel(dt_ref, a_ref, skip_ref, rows_ref, q_ref, b_ref, dec_ref, own_ref, rows_out):
    rows_out[...] = rows_ref[...]
    block_count = dt_ref.shape[1] // BLOCK
    diagonal = lax.broadcasted_iota(jnp.int32, (SLOT, SLOT), 0) == lax.broadcasted_iota(
        jnp.int32, (SLOT, SLOT), 1
    )

    def upright(row):
        return jnp.sum(jnp.where(diagonal, row, 0.0), axis=1, keepdims=True)

    rate = -jnp.exp(upright(a_ref[...]))
    upper = (
        lax.broadcasted_iota(jnp.int32, (BLOCK, BLOCK), 0)
        <= lax.broadcasted_iota(jnp.int32, (BLOCK, BLOCK), 1)
    ).astype(F32)
    prior = jnp.zeros((SLOT, 1), F32)
    later = jnp.zeros((SLOT, 1), F32)
    lane = lax.broadcasted_iota(jnp.int32, (SLOT, SLOT), 1)
    logs = jnp.zeros((SLOT, SLOT), F32)
    for c in range(block_count):
        columns = slice(c * BLOCK, (c + 1) * BLOCK)
        dt = dt_ref[:, columns]
        step = jnp.maximum(dt, 0.0) + jnp.log1p(jnp.exp(-jnp.abs(dt)))
        cum = jnp.dot(rate * step, upper, precision=HIGHEST, preferred_element_type=F32)
        last = cum[:, BLOCK - 1 : BLOCK]
        scaled = cum * LOG2E
        b_ref[:, columns] = scaled - jnp.log(step) * LOG2E
        parts = [scaled]
        parts.extend(split(jnp.exp(last - cum) * step))
        parts.extend(split(jnp.exp(cum)))
        parts.extend(split(jnp.exp(cum + prior)))
        parts.append(jnp.zeros_like(cum))
        q_ref[columns, :] = jnp.concatenate(parts, axis=0).T
        logs = jnp.where(lane == c, last, logs)
        logs = jnp.where(lane == block_count + c, later, logs)
        prior = prior + last
        if c > 0:
            later = later + last
    logs = jnp.where(lane == 2 * block_count, later, logs)
    logs = jnp.where(lane == SLOT - 1, prior, logs)
    factors = jnp.where(lane == 2 * block_count + 1, upright(skip_ref[...]), jnp.exp(logs))
    width = dec_ref.shape[1]
    head = lax.broadcasted_iota(jnp.int32, (SLOT, width), 1) // HEAD_DIM
    spread = (lax.broadcasted_iota(jnp.int32, (SLOT, width), 0) == head).astype(F32)
    rows = lax.dot_general(
        factors, spread, (((0,), (0,)), ((), ())), precision=HIGHEST, preferred_element_type=F32
    )
    dec_ref[...] = rows
    own_ref[...] = rows[SLOT - 1 : SLOT]


def rates(dt, a_log, d_skip, rows, width):
    length = dt.shape[1]
    return pl.pallas_call(
        rates_kernel,
        out_shape=[
            kept_in_vmem((length, 128), F32),
            kept_in_vmem((SLOT, length), F32),
            kept_in_vmem((SLOT, width), F32),
            kept_in_vmem((1, width), F32),
            jax.ShapeDtypeStruct(rows.shape, BF16),
        ],
        in_specs=[whole()] * 4,
        out_specs=[whole()] * 5,
        compiler_params=params(),
        cost_estimate=cost(0, 0),
    )(dt, a_log, d_skip, rows)


def expander(ref, slot, base):
    row = lax.broadcasted_iota(jnp.int32, ref.shape, 0)
    head = (lax.broadcasted_iota(jnp.int32, ref.shape, 1) + base) // HEAD_DIM
    ref[...] = ((row == slot * SLOT + head) | (row == (slot + 1) * SLOT + head)).astype(BF16)


def prepare_kernel(place_ref, bc_ref, b_ref, c_ref, place_out):
    rows = bc_ref.shape[0]
    for i in range(place_ref.shape[0]):
        place_out[i] = place_ref[i]
    b_ref[0:rows, :] = bc_ref[:, :STATE]
    b_ref[rows : rows + RIM, :] = bc_ref[rows - RIM :, STATE:]
    c_ref[...] = bc_ref[:, STATE:]


def prepare(place, bc_raw):
    rows = bc_raw.shape[0]
    return pl.pallas_call(
        prepare_kernel,
        out_shape=[
            jax.ShapeDtypeStruct((rows + RIM, STATE), BF16),
            jax.ShapeDtypeStruct((rows, STATE), BF16),
            pltpu.SMEM(place.shape, jnp.int32),
        ],
        in_specs=[whole(pltpu.SMEM), whole()],
        out_specs=[whole(), whole(), whole(pltpu.SMEM)],
        compiler_params=params(),
        cost_estimate=cost(0, 0),
    )(place, bc_raw)


def pack_kernel(count, *refs):
    out_ref = refs[-1]
    per = refs[0].shape[0]
    for i in range(count):
        out_ref[i * per : (i + 1) * per, :] = refs[i][...]


def pack(zones, *after):
    rows, columns = zones[0].shape
    return pl.pallas_call(
        functools.partial(pack_kernel, len(zones)),
        out_shape=jax.ShapeDtypeStruct((len(zones) * rows, columns), BF16),
        in_specs=[whole()] * len(zones) + [whole(pl.ANY)] * len(after),
        out_specs=whole(),
        compiler_params=params(),
        cost_estimate=cost(0, 0),
    )(*zones, *after)


def act_kernel(own_rows, plan, is_b, me_ref, weight_ref, bias_ref, *refs):
    sources = refs[: 1 + max(index for index, *_ in plan) + (not is_b)]
    act_ref, first_ref, last_ref, raw = refs[-4:]
    me = me_ref[0]
    size = act_ref.shape[0] // own_rows
    partner = me + 1 - 2 * lax.rem(me, 2)
    if is_b:
        raw[0:RIM, :] = jnp.zeros((RIM, STATE), BF16)
    else:
        raw[0:RIM, :] = sources[-1][RIM : 2 * RIM, :]
    for index, start, side, shift in plan:
        ref = sources[index]
        owner = lax.rem((partner if side else me) - 2 * shift + size, size)
        at = pl.multiple_of(RIM + owner * own_rows, 16)
        raw[pl.ds(at, own_rows), :] = ref[start : start + own_rows, :]
        if is_b:

            @pl.when(owner == size - 1)
            def _(ref=ref, start=start):
                end = start + own_rows
                last_ref[0:RIM, :] = ref[end - RIM : end, :]
                last_ref[RIM : 2 * RIM, :] = ref[end : end + RIM, :]

    first_ref[...] = raw[RIM : 2 * RIM, :]
    part = slice(0, STATE) if is_b else slice(STATE, 2 * STATE)
    weight = weight_ref[:, part]
    bias = bias_ref[:, part]
    for c in range(act_ref.shape[0] // BLOCK):
        slab = raw[c * BLOCK : c * BLOCK + RIM + BLOCK, :].astype(F32)
        act_ref[c * BLOCK : (c + 1) * BLOCK, :] = conv_slab(slab, weight, bias)


def activate(me, sources, plan, is_b, weight, bias, own_rows, after=()):
    length = len(plan) * own_rows
    return pl.pallas_call(
        functools.partial(act_kernel, own_rows, plan, is_b),
        out_shape=[
            kept_in_vmem((length, STATE), BF16),
            kept_in_vmem((RIM, STATE), BF16),
            kept_in_vmem((2 * RIM, STATE), BF16),
        ],
        in_specs=[whole(pltpu.SMEM)]
        + [whole()] * (len(sources) + 2)
        + [whole(pl.ANY)] * len(after),
        out_specs=[whole()] * 3,
        scratch_shapes=[pltpu.VMEM((RIM + length, STATE), BF16)],
        compiler_params=params(),
        cost_estimate=cost(0, 0),
    )(me, weight, bias, *sources, *after)


def tiles(width, step=512):
    step = min(step, width)
    return [slice(i, i + step) for i in range(0, width, step)]


def scale_kernel(x_ref, q_ref, first_ref, later_ref, expand_ref, held, sems):
    copies = stream_in(x_ref, held, sems)
    expander(expand_ref, 1, 0)
    for c, copy in enumerate(copies):
        rows = slice(c * BLOCK, (c + 1) * BLOCK)
        q_block = q_ref[rows, :].astype(BF16)
        copy.wait()
        for columns in tiles(x_ref.shape[1]):
            weight = jnp.dot(q_block, expand_ref[:, columns], preferred_element_type=F32)
            scaled = (held[c, :, columns].astype(F32) * weight).astype(BF16)
            if c == 0:
                first_ref[:, columns] = scaled
            else:
                later_ref[(c - 1) * BLOCK : c * BLOCK, columns] = scaled


def scale(x, q):
    length, width = x.shape
    count = length // BLOCK
    return pl.pallas_call(
        scale_kernel,
        out_shape=[
            kept_in_vmem((BLOCK, width), BF16),
            kept_in_vmem((length - BLOCK, width), BF16),
        ],
        in_specs=[whole(pltpu.HBM), whole()],
        out_specs=[whole()] * 2,
        scratch_shapes=[
            pltpu.VMEM((128, width), BF16),
            pltpu.VMEM((count, BLOCK, width), BF16),
            pltpu.SemaphoreType.DMA((count,)),
        ],
        compiler_params=params(),
        cost_estimate=cost(0, 0),
    )(x, q)


def block_state(b_block, scaled):
    return lax.dot_general(
        b_block, scaled, (((0,), (0,)), ((), ())), preferred_element_type=F32
    )


def later_states_kernel(b_ref, xs_ref, dec_ref, *refs):
    starts_ref, total_ref = refs[-2:]
    for c in range(1, b_ref.shape[0] // BLOCK):
        rows = slice(c * BLOCK, (c + 1) * BLOCK)
        b_block = b_ref[rows, :]
        for columns in tiles(xs_ref.shape[1]):
            state = block_state(b_block, xs_ref[(c - 1) * BLOCK : c * BLOCK, columns])
            if c == 1:
                starts_ref[0, :, columns] = jnp.zeros_like(state).astype(BF16)
                total_ref[:, columns] = state
            else:
                before = total_ref[:, columns]
                starts_ref[c - 1, :, columns] = before.astype(BF16)
                total_ref[:, columns] = dec_ref[c : c + 1, columns] * before + state


def later_states(b_act, xs, dec, after=()):
    length, width = xs.shape
    return pl.pallas_call(
        later_states_kernel,
        out_shape=[
            kept_in_vmem((length // BLOCK, STATE, width), BF16),
            kept_in_vmem((STATE, width), F32),
        ],
        in_specs=[whole()] * 3 + [whole(pl.ANY)] * len(after),
        out_specs=[whole()] * 2,
        compiler_params=params(),
        cost_estimate=cost(0, 0),
    )(b_act, xs, dec, *after)


def first_state_kernel(
    at_ref, b_ref, first_ref, rim_ref, weight_ref, bias_ref, xs_ref, dec_ref, later_ref, *refs
):
    b_out, state_ref, kept_ref, sent_ref, total_ref = refs[-5:]
    slab = jnp.concatenate([rim_ref[0:RIM, :], first_ref[...]], axis=0).astype(F32)
    fixed = conv_slab(slab, weight_ref[:, :STATE], bias_ref[:, :STATE])
    b_block = jnp.concatenate([fixed, b_ref[RIM:BLOCK, :]], axis=0)
    b_out[0:RIM, :] = fixed
    row = 2 * (b_out.shape[0] // BLOCK)
    for columns in tiles(xs_ref.shape[1]):
        state = block_state(b_block, xs_ref[0:BLOCK, columns])
        state_ref[:, columns] = state
        total = later_ref[:, columns] + dec_ref[row : row + 1, columns] * state
        total_ref[:, columns] = total.astype(BF16)
    half = kept_ref.shape[1]
    at = pl.multiple_of(at_ref[1], 128)
    kept_ref[...] = total_ref[:, pl.ds(at, half)]
    sent_ref[...] = total_ref[:, pl.ds(pl.multiple_of(half - at, 128), half)]


def first_state(at, b_act, first, rim, weight, bias, xs, dec, later, after=()):
    width = xs.shape[1]
    return pl.pallas_call(
        first_state_kernel,
        out_shape=[
            kept_in_vmem(b_act.shape, BF16),
            kept_in_vmem((STATE, width), F32),
            kept_in_vmem((STATE, width // 2), BF16),
            kept_in_vmem((STATE, width // 2), BF16),
        ],
        in_specs=[whole(pltpu.SMEM)] + [whole()] * 8 + [whole(pl.ANY)] * len(after),
        out_specs=[whole()] * 4,
        scratch_shapes=[pltpu.VMEM((STATE, width), BF16)],
        input_output_aliases={1: 0},
        compiler_params=params(),
        cost_estimate=cost(0, 0),
    )(at, b_act, first, rim, weight, bias, xs, dec, later, *after)


def meet_kernel(at_ref, kept_ref, got_ref, own_ref, partner_ref, out_ref):
    half = kept_ref.shape[1]
    columns = pl.ds(pl.multiple_of(at_ref[1], 128), half)
    odd = at_ref[1] == 0
    kept_decay = jnp.where(odd, 1.0, partner_ref[:, columns])
    got_decay = jnp.where(odd, own_ref[:, columns], 1.0)
    both = kept_decay * kept_ref[...].astype(F32) + got_decay * got_ref[...].astype(F32)
    out_ref[...] = both.astype(BF16)


def meet(at, kept, got, own, partner):
    return pl.pallas_call(
        meet_kernel,
        out_shape=kept_in_vmem(kept.shape, BF16),
        in_specs=[whole(pltpu.SMEM)] + [whole()] * 4,
        out_specs=whole(),
        compiler_params=params(),
        cost_estimate=cost(0, 0),
    )(at, kept, got, own, partner)


def arrive_kernel(at_ref, crossed_ref, kept_ref, got_ref, own_ref, partner_ref, *refs):
    in_ref, sent_ref = refs[-2:]
    half = kept_ref.shape[1]
    columns = pl.ds(pl.multiple_of(at_ref[1], 128), half)
    odd = at_ref[1] == 0
    decay = jnp.where(odd, partner_ref[:, columns], own_ref[:, columns])
    crossed = crossed_ref[...]
    mine = jnp.where(odd, got_ref[...].astype(F32), kept_ref[...].astype(F32))
    after_even = (decay * crossed.astype(F32) + mine).astype(BF16)
    in_ref[...] = jnp.where(odd, after_even, crossed)
    sent_ref[...] = jnp.where(odd, crossed, after_even)


def arrive(at, crossed, kept, got, own, partner, after):
    return pl.pallas_call(
        arrive_kernel,
        out_shape=[kept_in_vmem(kept.shape, BF16)] * 2,
        in_specs=[whole(pltpu.SMEM)] + [whole()] * 5 + [whole(pl.ANY)],
        out_specs=[whole()] * 2,
        compiler_params=params(),
        cost_estimate=cost(0, 0),
    )(at, crossed, kept, got, own, partner, after)


def inner_kernel(
    c_ref, b_ref, x_ref, z_ref, q_ref, brow_ref, starts_ref, state_ref, dec_ref,
    out_ref, z_out, expand_ref, held, sems, z_sem,
):
    stream_in(x_ref, held, sems)
    z_copy = pltpu.make_async_copy(z_ref, z_out, z_sem)
    z_copy.start()
    half = BLOCK // 2
    block_count = x_ref.shape[0] // BLOCK
    head_count = x_ref.shape[1] // HEAD_DIM
    expander(expand_ref, 3, 0)
    lower = lax.broadcasted_iota(jnp.int32, (half, half), 0) >= lax.broadcasted_iota(
        jnp.int32, (half, half), 1
    )

    @pl.loop(0, block_count)
    def _(c):
        at = pl.multiple_of(c * BLOCK, BLOCK)
        rows = pl.ds(at, BLOCK)
        pltpu.make_async_copy(x_ref.at[rows, :], held.at[c], sems.at[c]).wait()
        c_block = c_ref[rows, :]
        gram = lax.dot_general(
            c_block, b_ref[rows, :], (((1,), (1,)), ((), ())), preferred_element_type=F32
        )
        gram_00 = jnp.where(lower, gram[:half, :half], 0.0)
        gram_10 = gram[half:, :half]
        gram_11 = jnp.where(lower, gram[half:, half:], 0.0)
        q_block = q_ref[rows, :]
        q_short = q_block.astype(BF16)
        for h in range(head_count):
            columns = slice(h * HEAD_DIM, (h + 1) * HEAD_DIM)
            rise = jnp.broadcast_to(q_block[:, h : h + 1], (BLOCK, half))
            fall = brow_ref[h : h + 1, rows]
            w_00 = gram_00 * jnp.exp2(jnp.minimum(rise[:half] - fall[:, :half], 120.0))
            w_10 = gram_10 * jnp.exp2(rise[half:] - fall[:, :half])
            w_11 = gram_11 * jnp.exp2(jnp.minimum(rise[half:] - fall[:, half:], 120.0))
            x_head = held[c, :, columns]
            top = jnp.dot(w_00.astype(BF16), x_head[:half], preferred_element_type=F32)
            low = jnp.concatenate([w_10.astype(BF16), w_11.astype(BF16)], axis=1)
            bottom = jnp.dot(low, x_head, preferred_element_type=F32)
            out_ref[rows, columns] = jnp.concatenate([top, bottom], axis=0) + dec_ref[
                2 * block_count + 1 : 2 * block_count + 2, columns
            ] * x_head.astype(F32)

        @pl.when(c > 0)
        def _():
            for columns in tiles(x_ref.shape[1]):
                decay = dec_ref[pl.ds(block_count + c, 1), columns]
                start = starts_ref[c - 1, :, columns].astype(F32) + decay * state_ref[:, columns]
                grown = jnp.dot(q_short, expand_ref[:, columns], preferred_element_type=F32)
                carried = jnp.dot(c_block, start.astype(BF16), preferred_element_type=F32)
                out_ref[rows, columns] += grown * carried

    z_copy.wait()


def inner(c_act, b_act, x, z, q, brow, starts, state, dec):
    length, width = x.shape
    return pl.pallas_call(
        inner_kernel,
        out_shape=[kept_in_vmem((length, width), F32), kept_in_vmem(z.shape, z.dtype)],
        in_specs=[whole()] * 2 + [whole(pltpu.HBM)] * 2 + [whole()] * 5,
        out_specs=[whole()] * 2,
        scratch_shapes=[
            pltpu.VMEM((128, width), BF16),
            pltpu.VMEM((length // BLOCK, BLOCK, width), BF16),
            pltpu.SemaphoreType.DMA((length // BLOCK,)),
            pltpu.SemaphoreType.DMA,
        ],
        compiler_params=params(),
        cost_estimate=cost(0, 13 * length * width),
    )(c_act, b_act, x, z, q, brow, starts, state, dec)


def gate_kernel(second, at_ref, c_ref, y_ref, z_ref, q_ref, in_ref, *refs):
    out_ref, sum_ref, expand_ref, squares_ref = refs[-4:]
    width = in_ref.shape[1]
    base = pl.multiple_of(width - at_ref[1] if second else at_ref[1], 128)
    expander(expand_ref, 5, base)
    blocks = [slice(c, c + BLOCK) for c in range(0, y_ref.shape[0], BLOCK)]
    for rows in blocks:
        c_block = c_ref[rows, :]
        q_short = q_ref[rows, :].astype(BF16)
        squares = None
        for part in tiles(width, 256):
            size = part.stop - part.start
            columns = pl.ds(pl.multiple_of(base + part.start, 128), size)
            grown = jnp.dot(q_short, expand_ref[:, part], preferred_element_type=F32)
            carried = jnp.dot(c_block, in_ref[:, part], preferred_element_type=F32)
            gated = (y_ref[rows, columns] + grown * carried) * silu(z_ref[rows, columns].astype(F32))
            out_ref[rows, columns] = gated
            square = gated * gated
            for i in range(0, size, 128):
                one = square[:, i : i + 128]
                squares = one if squares is None else squares + one
        squares_ref[rows, :] = squares
    for rows in blocks:
        total = jnp.sum(squares_ref[rows, :].T, axis=0, keepdims=True)
        sum_ref[:, rows] = refs[0][:, rows] + total if second else total


def gate(at, c_act, y, z, q, incoming, *before):
    length, width = y.shape
    return pl.pallas_call(
        functools.partial(gate_kernel, len(before) > 0),
        out_shape=[
            kept_in_vmem((length, width), F32),
            kept_in_vmem((1, length), F32),
        ],
        in_specs=[whole(pltpu.SMEM)] + [whole()] * (5 + len(before)),
        out_specs=[whole()] * 2,
        scratch_shapes=[
            pltpu.VMEM((128, incoming.shape[1]), BF16),
            pltpu.VMEM((length, 128), F32),
        ],
        input_output_aliases={2: 0},
        compiler_params=params(),
        cost_estimate=cost(0, 8 * length * width),
    )(at, c_act, y, z, q, incoming, *before)


def norm_kernel(g_ref, one_ref, two_ref, gain_ref, out_ref, held, sems):
    copies = []
    for c in range(g_ref.shape[0] // BLOCK):
        rows = slice(c * BLOCK, (c + 1) * BLOCK)
        square_sum = one_ref[:, rows] + two_ref[:, rows]
        inverse = lax.rsqrt(square_sum / INNER + 1e-05)
        scale = jnp.broadcast_to(inverse, (128, BLOCK)).T
        for i in range(0, g_ref.shape[1], 128):
            columns = slice(i, i + 128)
            held[c, :, columns] = (g_ref[rows, columns] * scale * gain_ref[:, columns]).astype(BF16)
        copy = pltpu.make_async_copy(held.at[c], out_ref.at[rows, :], sems.at[c])
        copy.start()
        copies.append(copy)
    for copy in copies:
        copy.wait()


def norm(gated, one, two, gain):
    length, width = gated.shape
    count = length // BLOCK
    return pl.pallas_call(
        norm_kernel,
        out_shape=jax.ShapeDtypeStruct((length, width), BF16),
        in_specs=[whole()] * 4,
        out_specs=whole(pltpu.HBM),
        scratch_shapes=[
            pltpu.VMEM((count, BLOCK, width), BF16),
            pltpu.SemaphoreType.DMA((count,)),
        ],
        compiler_params=params(),
        cost_estimate=cost(0, 0),
    )(gated, one, two, gain)


SWAP = [(0, 1), (1, 0), (2, 3), (3, 2)]


def zone_shift(a, k):
    size = lax.axis_size("head")
    return lax.ppermute(a, "head", [(i, (i + 2 * k) % size) for i in range(size)])


def side_swap(a):
    size = lax.axis_size("head")
    return lax.ppermute(a, "head", [(i, i ^ 1) for i in range(size)])


def chained_state(at, kept, sent, own, partner, after):
    size = lax.axis_size("seq")
    if size == 4:
        got = lax.ppermute(sent, "seq", SWAP)
        both = meet(at, kept, got, own, partner)
        crossed = lax.ppermute(both, "seq", [(0, 2), (1, 3)])
        mine, passed = arrive(at, crossed, kept, got, own, partner, after)
        return mine, lax.ppermute(passed, "seq", SWAP)
    totals = lax.all_gather(jnp.concatenate([kept, sent], axis=1), "seq")
    decays = lax.all_gather(own, "seq")

    def one(hop, state):
        decay = lax.dynamic_index_in_dim(decays, hop, 0, False)
        return decay * state + lax.dynamic_index_in_dim(totals, hop, 0, False).astype(F32)

    place = lax.axis_index("seq")
    state = lax.fori_loop(0, place, one, jnp.zeros(totals.shape[1:], F32)).astype(BF16)
    half = kept.shape[1]
    return state[:, :half], state[:, half:]


def on_device(x_inner, z_gate, bc_raw, conv_weight, conv_bias, dt_raw, a_log, d_skip, norm_gain):
    x_inner, z_gate = in_hbm(x_inner), in_hbm(z_gate)
    head_count = a_log.shape[0]
    own_rows = bc_raw.shape[0]
    seq_size = lax.axis_size("seq")
    shifts = range(1, lax.axis_size("head") // 2)
    width = x_inner.shape[1]
    first_channel = 0
    if seq_size == 4:
        first_channel = (1 - lax.rem(lax.axis_index("seq"), 2)) * (width // 2)
    place = jnp.stack([lax.axis_index("head"), first_channel]).astype(jnp.int32)
    own_b, own_c, place = prepare(place, bc_raw)
    zones_b = [zone_shift(own_b, k) for k in shifts]
    side_b = side_swap(own_b)
    pad = SLOT - head_count
    q, brow, dec, own_decay, own_c = rates(
        jnp.pad(dt_raw.T, ((0, pad), (0, 0))),
        jnp.pad(a_log, (0, pad))[None, :],
        jnp.pad(d_skip, (0, pad))[None, :],
        own_c,
        width,
    )
    zones_c = [zone_shift(own_c, k) for k in shifts]
    side_c = side_swap(own_c)
    others_b = side_swap(pack(zones_b, own_decay, side_b))
    others_c = side_swap(pack(zones_c, side_c))

    def plan(per):
        first = [(0, 0, False, 0), (1, 0, True, 0)]
        near = [(k + 1, 0, False, k) for k in shifts]
        return first + near + [(len(near) + 2, (k - 1) * per, True, k) for k in shifts]

    plan_b, plan_c = plan(own_b.shape[0]), plan(own_rows)
    sources_b = [own_b, side_b, *zones_b, others_b]
    sources_c = [own_c, side_c, *zones_c, others_c]
    bias = conv_bias[None, :]
    xs_first, xs_later = scale(x_inner, q)
    partner_decay = own_decay
    if seq_size == 4:
        partner_decay = lax.ppermute(own_decay, "seq", SWAP)
    b_act, first_b, last_rows = activate(
        place, sources_b, plan_b, True, conv_weight, bias, own_rows, [xs_first]
    )
    rims = lax.ppermute(last_rows, "seq", [(i, i + 1) for i in range(seq_size - 1)])
    starts, later = later_states(b_act, xs_later, dec)
    b_act, state_0, kept, sent = first_state(
        place, b_act, first_b, rims, conv_weight, bias, xs_first, dec, later, [others_c]
    )
    c_act, _, _ = activate(place, [*sources_c, rims], plan_c, False, conv_weight, bias, own_rows)
    local, z_held = inner(c_act, b_act, x_inner, z_gate, q, brow, starts, state_0, dec)
    state_one, state_two = chained_state(place, kept, sent, own_decay, partner_decay, local)
    gated, square_one = gate(place, c_act, local, z_held, q, state_one)
    gated, square_sum = gate(place, c_act, gated, z_held, q, state_two, square_one)
    column = sum([zone_shift(square_sum, k) for k in shifts], square_sum)
    return norm(gated, column, side_swap(column), norm_gain[None, :])


def solution(mesh):
    placed = (
        P("seq", "head"),
        P("seq", "head"),
        P(("seq", "head"), None),
        P(),
        P(),
        P("seq", "head"),
        P("head"),
        P("head"),
        P("head"),
    )
    return jax.shard_map(
        on_device, mesh=mesh, in_specs=placed, out_specs=P("seq", "head"), check_vma=False
    )
```

```python
import functools
import math

import jax
import jax.numpy as jnp
from jax import lax
from jax.experimental import pallas as pl
from jax.experimental.pallas import tpu as pltpu
from jax.sharding import PartitionSpec as P

HEAD_DIM = 128
STATE = 256
BLOCK = 256
INNER = 16384
RIM = 16
SLOT = 16
PIECES = 4
LOG2E = math.log2(math.e)
F32 = jnp.float32
BF16 = jnp.bfloat16
HIGHEST = lax.Precision.HIGHEST
VMEM_LIMIT = 14 * 1024 * 1024


def params():
    return pltpu.CompilerParams(vmem_limit_bytes=VMEM_LIMIT)


def whole(memory_space=pltpu.VMEM):
    return pl.BlockSpec(memory_space=memory_space)


def kept_in_vmem(shape, dtype):
    return pltpu.VMEM(shape, dtype)


def stream_in(hbm_ref, held, sems, columns=None):
    copies = []
    for c in range(held.shape[0]):
        rows = pl.ds(c * BLOCK, BLOCK)
        source = hbm_ref.at[rows, :] if columns is None else hbm_ref.at[rows, columns]
        copy = pltpu.make_async_copy(source, held.at[c], sems.at[c])
        copy.start()
        copies.append(copy)
    return copies


def in_hbm(a):
    return pltpu.with_memory_space_constraint(a, pltpu.HBM)


def cost(flops, nbytes, trans=0):
    return pl.CostEstimate(flops=int(flops), bytes_accessed=int(nbytes), transcendentals=int(trans))


def silu(v):
    half = 0.5 * v
    return half + half * jnp.tanh(half)


def split(v):
    high = v.astype(BF16).astype(F32)
    return high, v - high


def conv_slab(slab, weight, bias):
    taps = weight.shape[0]
    total = jnp.broadcast_to(bias, slab.shape)
    for k in range(taps):
        shift = taps - 1 - k
        moved = pltpu.roll(slab, shift, 0) if shift else slab
        total = total + weight[k : k + 1, :] * moved
    total = total[RIM:]
    return (total * jax.nn.sigmoid(total)).astype(BF16)


def rates_kernel(
    dt_hbm, a_ref, skip_ref, x_ref, q_ref, b_ref, dec_ref, own_ref, first_ref, later_ref,
    dt_ref, expand_ref, held, sems, dt_sem,
):
    dt_copy = pltpu.make_async_copy(dt_hbm, dt_ref, dt_sem)
    dt_copy.start()
    copies = stream_in(x_ref, held, sems)
    expander(expand_ref, 1, 0)
    block_count = dt_ref.shape[1] // BLOCK
    diagonal = lax.broadcasted_iota(jnp.int32, (SLOT, SLOT), 0) == lax.broadcasted_iota(
        jnp.int32, (SLOT, SLOT), 1
    )

    def upright(row):
        return jnp.sum(jnp.where(diagonal, row, 0.0), axis=1, keepdims=True)

    rate = -jnp.exp(upright(a_ref[...]))
    upper = (
        lax.broadcasted_iota(jnp.int32, (BLOCK, BLOCK), 0)
        <= lax.broadcasted_iota(jnp.int32, (BLOCK, BLOCK), 1)
    ).astype(F32)
    prior = jnp.zeros((SLOT, 1), F32)
    later = jnp.zeros((SLOT, 1), F32)
    lane = lax.broadcasted_iota(jnp.int32, (SLOT, SLOT), 1)
    logs = jnp.zeros((SLOT, SLOT), F32)
    dt_copy.wait()
    for c in range(block_count):
        columns = slice(c * BLOCK, (c + 1) * BLOCK)
        dt = dt_ref[:, columns]
        step = jnp.maximum(dt, 0.0) + jnp.log1p(jnp.exp(-jnp.abs(dt)))
        cum = jnp.dot(rate * step, upper, precision=HIGHEST, preferred_element_type=F32)
        last = cum[:, BLOCK - 1 : BLOCK]
        scaled = cum * LOG2E
        b_ref[:, columns] = scaled - jnp.log(step) * LOG2E
        parts = [scaled]
        parts.extend(split(jnp.exp(last - cum) * step))
        parts.extend(split(jnp.exp(cum)))
        parts.extend(split(jnp.exp(cum + prior)))
        parts.append(jnp.zeros_like(cum))
        q_ref[columns, :] = jnp.concatenate(parts, axis=0).T
        logs = jnp.where(lane == c, last, logs)
        logs = jnp.where(lane == block_count + c, later, logs)
        prior = prior + last
        if c > 0:
            later = later + last
    logs = jnp.where(lane == 2 * block_count, later, logs)
    logs = jnp.where(lane == SLOT - 1, prior, logs)
    factors = jnp.where(lane == 2 * block_count + 1, upright(skip_ref[...]), jnp.exp(logs))
    width = dec_ref.shape[1]
    head = lax.broadcasted_iota(jnp.int32, (SLOT, width), 1) // HEAD_DIM
    spread = (lax.broadcasted_iota(jnp.int32, (SLOT, width), 0) == head).astype(F32)
    rows = lax.dot_general(
        factors, spread, (((0,), (0,)), ((), ())), precision=HIGHEST, preferred_element_type=F32
    )
    dec_ref[...] = rows
    own_ref[...] = rows[SLOT - 1 : SLOT]
    for copy in copies:
        copy.wait()
    for c in range(block_count):
        rows = slice(c * BLOCK, (c + 1) * BLOCK)
        q_block = q_ref[rows, :].astype(BF16)
        for columns in tiles(width):
            weight = jnp.dot(q_block, expand_ref[:, columns], preferred_element_type=F32)
            scaled = (held[c, :, columns].astype(F32) * weight).astype(BF16)
            if c == 0:
                first_ref[:, columns] = scaled
            else:
                later_ref[(c - 1) * BLOCK : c * BLOCK, columns] = scaled


def rates(dt, a_log, d_skip, x):
    length, width = x.shape
    count = length // BLOCK
    return pl.pallas_call(
        rates_kernel,
        out_shape=[
            kept_in_vmem((length, 128), F32),
            kept_in_vmem((SLOT, length), F32),
            kept_in_vmem((SLOT, width), F32),
            kept_in_vmem((1, width), F32),
            kept_in_vmem((BLOCK, width), BF16),
            kept_in_vmem((length - BLOCK, width), BF16),
        ],
        in_specs=[whole(pltpu.HBM), whole(), whole(), whole(pltpu.HBM)],
        out_specs=[whole()] * 6,
        scratch_shapes=[
            pltpu.VMEM(dt.shape, F32),
            pltpu.VMEM((128, width), BF16),
            pltpu.VMEM((count, BLOCK, width), BF16),
            pltpu.SemaphoreType.DMA((count,)),
            pltpu.SemaphoreType.DMA,
        ],
        compiler_params=params(),
        cost_estimate=cost(0, 0),
    )(in_hbm(dt), a_log, d_skip, x)


def expander(ref, slot, base):
    row = lax.broadcasted_iota(jnp.int32, ref.shape, 0)
    head = (lax.broadcasted_iota(jnp.int32, ref.shape, 1) + base) // HEAD_DIM
    ref[...] = ((row == slot * SLOT + head) | (row == (slot + 1) * SLOT + head)).astype(BF16)


def prepare_kernel(place_ref, bc_ref, b_ref, c_ref, place_out, sems):
    rows = bc_ref.shape[0]
    copies = [
        pltpu.make_async_copy(bc_ref.at[:, 0:STATE], b_ref.at[0:rows, :], sems.at[0]),
        pltpu.make_async_copy(
            bc_ref.at[rows - RIM : rows, STATE : 2 * STATE], b_ref.at[rows : rows + RIM, :], sems.at[1]
        ),
        pltpu.make_async_copy(bc_ref.at[:, STATE : 2 * STATE], c_ref, sems.at[2]),
    ]
    for copy in copies:
        copy.start()
    for i in range(place_ref.shape[0]):
        place_out[i] = place_ref[i]
    for copy in copies:
        copy.wait()


def prepare(place, bc_raw):
    rows = bc_raw.shape[0]
    return pl.pallas_call(
        prepare_kernel,
        out_shape=[
            jax.ShapeDtypeStruct((rows + RIM, STATE), BF16),
            jax.ShapeDtypeStruct((rows, STATE), BF16),
            pltpu.SMEM(place.shape, jnp.int32),
        ],
        in_specs=[whole(pltpu.SMEM), whole(pltpu.HBM)],
        out_specs=[whole(), whole(), whole(pltpu.SMEM)],
        scratch_shapes=[pltpu.SemaphoreType.DMA((3,))],
        compiler_params=params(),
        cost_estimate=cost(0, 0),
    )(place, in_hbm(bc_raw))


def pack_kernel(count, *refs):
    own_ref, side_ref = refs[count : count + 2]
    cat_ref, pair_ref = refs[-2:]
    per = refs[0].shape[0]
    for i in range(count):
        cat_ref[i * per : (i + 1) * per, :] = refs[i][...]
    rows = own_ref.shape[0]
    pair_ref[0:rows, :] = own_ref[...]
    pair_ref[rows : 2 * rows, :] = side_ref[...]


def pack(zones, own, side, *after):
    rows, columns = zones[0].shape
    return pl.pallas_call(
        functools.partial(pack_kernel, len(zones)),
        out_shape=[
            jax.ShapeDtypeStruct((len(zones) * rows, columns), BF16),
            jax.ShapeDtypeStruct((2 * own.shape[0], columns), BF16),
        ],
        in_specs=[whole()] * (len(zones) + 2) + [whole(pl.ANY)] * len(after),
        out_specs=[whole()] * 2,
        compiler_params=params(),
        cost_estimate=cost(0, 0),
    )(*zones, own, side, *after)


def act_kernel(own_rows, plan, is_b, me_ref, weight_ref, bias_ref, *refs):
    sources = refs[: 1 + max(index for index, *_ in plan) + (not is_b)]
    act_ref, first_ref, last_ref, raw = refs[-4:]
    me = me_ref[0]
    size = act_ref.shape[0] // own_rows
    partner = me + 1 - 2 * lax.rem(me, 2)
    if is_b:
        raw[0:RIM, :] = jnp.zeros((RIM, STATE), BF16)
    else:
        raw[0:RIM, :] = sources[-1][RIM : 2 * RIM, :]
    for index, start, side, shift in plan:
        ref = sources[index]
        owner = lax.rem((partner if side else me) - 2 * shift + size, size)
        at = pl.multiple_of(RIM + owner * own_rows, 16)
        raw[pl.ds(at, own_rows), :] = ref[start : start + own_rows, :]
        if is_b:

            @pl.when(owner == size - 1)
            def _(ref=ref, start=start):
                end = start + own_rows
                last_ref[0:RIM, :] = ref[end - RIM : end, :]
                last_ref[RIM : 2 * RIM, :] = ref[end : end + RIM, :]

    first_ref[...] = raw[RIM : 2 * RIM, :]
    part = slice(0, STATE) if is_b else slice(STATE, 2 * STATE)
    weight = weight_ref[:, part]
    bias = bias_ref[:, part]
    for c in range(act_ref.shape[0] // BLOCK):
        slab = raw[c * BLOCK : c * BLOCK + RIM + BLOCK, :].astype(F32)
        act_ref[c * BLOCK : (c + 1) * BLOCK, :] = conv_slab(slab, weight, bias)


def activate(me, sources, plan, is_b, weight, bias, own_rows, after=()):
    length = len(plan) * own_rows
    return pl.pallas_call(
        functools.partial(act_kernel, own_rows, plan, is_b),
        out_shape=[
            kept_in_vmem((length, STATE), BF16),
            kept_in_vmem((RIM, STATE), BF16),
            kept_in_vmem((2 * RIM, STATE), BF16),
        ],
        in_specs=[whole(pltpu.SMEM)]
        + [whole()] * (len(sources) + 2)
        + [whole(pl.ANY)] * len(after),
        out_specs=[whole()] * 3,
        scratch_shapes=[pltpu.VMEM((RIM + length, STATE), BF16)],
        compiler_params=params(),
        cost_estimate=cost(0, 0),
    )(me, weight, bias, *sources, *after)


def tiles(width, step=512):
    step = min(step, width)
    return [slice(i, i + step) for i in range(0, width, step)]


def block_state(b_block, scaled):
    return lax.dot_general(
        b_block, scaled, (((0,), (0,)), ((), ())), preferred_element_type=F32
    )


def later_states_kernel(b_ref, xs_ref, dec_ref, *refs):
    starts_ref, total_ref = refs[-2:]
    for c in range(1, b_ref.shape[0] // BLOCK):
        rows = slice(c * BLOCK, (c + 1) * BLOCK)
        b_block = b_ref[rows, :]
        for columns in tiles(xs_ref.shape[1]):
            state = block_state(b_block, xs_ref[(c - 1) * BLOCK : c * BLOCK, columns])
            if c == 1:
                starts_ref[0, :, columns] = jnp.zeros_like(state).astype(BF16)
                total_ref[:, columns] = state
            else:
                before = total_ref[:, columns]
                starts_ref[c - 1, :, columns] = before.astype(BF16)
                total_ref[:, columns] = dec_ref[c : c + 1, columns] * before + state


def later_states(b_act, xs, dec, after=()):
    length, width = xs.shape
    return pl.pallas_call(
        later_states_kernel,
        out_shape=[
            kept_in_vmem((length // BLOCK, STATE, width), BF16),
            kept_in_vmem((STATE, width), F32),
        ],
        in_specs=[whole()] * 3 + [whole(pl.ANY)] * len(after),
        out_specs=[whole()] * 2,
        compiler_params=params(),
        cost_estimate=cost(0, 0),
    )(b_act, xs, dec, *after)


def first_state_kernel(
    at_ref, b_ref, first_ref, rim_ref, weight_ref, bias_ref, xs_ref, dec_ref, later_ref, *refs
):
    own_ref, b_out, state_ref, kept_ref, *sent_refs, total_ref = refs
    slab = jnp.concatenate([rim_ref[0:RIM, :], first_ref[...]], axis=0).astype(F32)
    fixed = conv_slab(slab, weight_ref[:, :STATE], bias_ref[:, :STATE])
    b_block = jnp.concatenate([fixed, b_ref[RIM:BLOCK, :]], axis=0)
    b_out[0:RIM, :] = fixed
    row = 2 * (b_out.shape[0] // BLOCK)
    for columns in tiles(xs_ref.shape[1]):
        state = block_state(b_block, xs_ref[0:BLOCK, columns])
        state_ref[:, columns] = state
        total = later_ref[:, columns] + dec_ref[row : row + 1, columns] * state
        total_ref[:, columns] = total.astype(BF16)
    half = kept_ref.shape[1]
    at = pl.multiple_of(at_ref[1], 128)
    kept_ref[...] = total_ref[:, pl.ds(at, half)]
    size = half // len(sent_refs)
    row_index = lax.broadcasted_iota(jnp.int32, (RIM, size), 0)
    for i, sent_ref in enumerate(sent_refs):
        columns = pl.ds(pl.multiple_of(half - at + i * size, 128), size)
        sent_ref[0:STATE, :] = total_ref[:, columns]
        rest = own_ref[:, columns]
        rows = jnp.zeros((RIM, size), F32)
        for k in range(3):
            term = rest.astype(BF16).astype(F32)
            rows = jnp.where(row_index == k, term, rows)
            rest = rest - term
        sent_ref[STATE : STATE + RIM, :] = rows.astype(BF16)


def first_state(at, b_act, first, rim, weight, bias, xs, dec, later, own):
    width = xs.shape[1]
    pieces = PIECES if width >= 256 * PIECES else 1
    return pl.pallas_call(
        first_state_kernel,
        out_shape=[
            kept_in_vmem(b_act.shape, BF16),
            kept_in_vmem((STATE, width), F32),
            kept_in_vmem((STATE, width // 2), BF16),
        ]
        + [kept_in_vmem((STATE + RIM, width // 2 // pieces), BF16)] * pieces,
        in_specs=[whole(pltpu.SMEM)] + [whole()] * 9,
        out_specs=[whole()] * (3 + pieces),
        scratch_shapes=[pltpu.VMEM((STATE, width), BF16)],
        input_output_aliases={1: 0},
        compiler_params=params(),
        cost_estimate=cost(0, 0),
    )(at, b_act, first, rim, weight, bias, xs, dec, later, own)


def meet_kernel(count, at_ref, kept_ref, own_ref, *refs):
    got_refs = refs[:count]
    out_ref, got_ref, partner_ref = refs[-3:]
    size = got_refs[0].shape[1]
    for i, ref in enumerate(got_refs):
        part = slice(i * size, (i + 1) * size)
        got_ref[:, part] = ref[0:STATE, :]
        rows = ref[STATE : STATE + RIM, :].astype(F32)
        partner_ref[:, part] = rows[0:1] + rows[1:2] + rows[2:3]
    half = kept_ref.shape[1]
    columns = pl.ds(pl.multiple_of(at_ref[1], 128), half)
    odd = at_ref[1] == 0
    kept_decay = jnp.where(odd, 1.0, partner_ref[...])
    got_decay = jnp.where(odd, own_ref[:, columns], 1.0)
    both = kept_decay * kept_ref[...].astype(F32) + got_decay * got_ref[...].astype(F32)
    out_ref[...] = both.astype(BF16)


def meet(at, kept, own, got, after):
    return pl.pallas_call(
        functools.partial(meet_kernel, len(got)),
        out_shape=[kept_in_vmem(kept.shape, BF16)] * 2
        + [kept_in_vmem((1, kept.shape[1]), F32)],
        in_specs=[whole(pltpu.SMEM)]
        + [whole()] * (2 + len(got))
        + [whole(pl.ANY)] * len(after),
        out_specs=[whole()] * 3,
        compiler_params=params(),
        cost_estimate=cost(0, 0),
    )(at, kept, own, *got, *after)


def arrive_kernel(at_ref, crossed_ref, kept_ref, got_ref, own_ref, partner_ref, *refs):
    in_ref, sent_ref = refs[-2:]
    half = kept_ref.shape[1]
    columns = pl.ds(pl.multiple_of(at_ref[1], 128), half)
    odd = at_ref[1] == 0
    decay = jnp.where(odd, partner_ref[...], own_ref[:, columns])
    crossed = crossed_ref[...]
    mine = jnp.where(odd, got_ref[...].astype(F32), kept_ref[...].astype(F32))
    after_even = (decay * crossed.astype(F32) + mine).astype(BF16)
    in_ref[...] = jnp.where(odd, after_even, crossed)
    sent_ref[...] = jnp.where(odd, crossed, after_even)


def arrive(at, crossed, kept, got, own, partner, after):
    return pl.pallas_call(
        arrive_kernel,
        out_shape=[kept_in_vmem(kept.shape, BF16)] * 2,
        in_specs=[whole(pltpu.SMEM)] + [whole()] * 5 + [whole(pl.ANY)],
        out_specs=[whole()] * 2,
        compiler_params=params(),
        cost_estimate=cost(0, 0),
    )(at, crossed, kept, got, own, partner, after)


def inner_kernel(
    c_ref, b_ref, x_ref, z_ref, q_ref, brow_ref, starts_ref, state_ref, dec_ref,
    out_ref, z_out, expand_ref, held, sems, z_sem,
):
    stream_in(x_ref, held, sems)
    z_copy = pltpu.make_async_copy(z_ref, z_out, z_sem)
    z_copy.start()
    half = BLOCK // 2
    block_count = x_ref.shape[0] // BLOCK
    head_count = x_ref.shape[1] // HEAD_DIM
    expander(expand_ref, 3, 0)
    lower = lax.broadcasted_iota(jnp.int32, (half, half), 0) >= lax.broadcasted_iota(
        jnp.int32, (half, half), 1
    )

    @pl.loop(0, block_count)
    def _(c):
        at = pl.multiple_of(c * BLOCK, BLOCK)
        rows = pl.ds(at, BLOCK)
        pltpu.make_async_copy(x_ref.at[rows, :], held.at[c], sems.at[c]).wait()
        c_block = c_ref[rows, :]
        gram = lax.dot_general(
            c_block, b_ref[rows, :], (((1,), (1,)), ((), ())), preferred_element_type=F32
        )
        gram_00 = jnp.where(lower, gram[:half, :half], 0.0)
        gram_10 = gram[half:, :half]
        gram_11 = jnp.where(lower, gram[half:, half:], 0.0)
        q_block = q_ref[rows, :]
        q_short = q_block.astype(BF16)
        for h in range(head_count):
            columns = slice(h * HEAD_DIM, (h + 1) * HEAD_DIM)
            rise = jnp.broadcast_to(q_block[:, h : h + 1], (BLOCK, half))
            fall = brow_ref[h : h + 1, rows]
            w_00 = gram_00 * jnp.exp2(jnp.minimum(rise[:half] - fall[:, :half], 120.0))
            w_10 = gram_10 * jnp.exp2(rise[half:] - fall[:, :half])
            w_11 = gram_11 * jnp.exp2(jnp.minimum(rise[half:] - fall[:, half:], 120.0))
            x_head = held[c, :, columns]
            top = jnp.dot(w_00.astype(BF16), x_head[:half], preferred_element_type=F32)
            low = jnp.concatenate([w_10.astype(BF16), w_11.astype(BF16)], axis=1)
            bottom = jnp.dot(low, x_head, preferred_element_type=F32)
            out_ref[rows, columns] = jnp.concatenate([top, bottom], axis=0) + dec_ref[
                2 * block_count + 1 : 2 * block_count + 2, columns
            ] * x_head.astype(F32)

        @pl.when(c > 0)
        def _():
            for columns in tiles(x_ref.shape[1]):
                decay = dec_ref[pl.ds(block_count + c, 1), columns]
                start = starts_ref[c - 1, :, columns].astype(F32) + decay * state_ref[:, columns]
                grown = jnp.dot(q_short, expand_ref[:, columns], preferred_element_type=F32)
                carried = jnp.dot(c_block, start.astype(BF16), preferred_element_type=F32)
                out_ref[rows, columns] += grown * carried

    z_copy.wait()


def inner(c_act, b_act, x, z, q, brow, starts, state, dec):
    length, width = x.shape
    return pl.pallas_call(
        inner_kernel,
        out_shape=[kept_in_vmem((length, width), F32), kept_in_vmem(z.shape, z.dtype)],
        in_specs=[whole()] * 2 + [whole(pltpu.HBM)] * 2 + [whole()] * 5,
        out_specs=[whole()] * 2,
        scratch_shapes=[
            pltpu.VMEM((128, width), BF16),
            pltpu.VMEM((length // BLOCK, BLOCK, width), BF16),
            pltpu.SemaphoreType.DMA((length // BLOCK,)),
            pltpu.SemaphoreType.DMA,
        ],
        compiler_params=params(),
        cost_estimate=cost(0, 80 * length * width),
    )(c_act, b_act, x, z, q, brow, starts, state, dec)


def gate_kernel(second, at_ref, c_ref, y_ref, z_ref, q_ref, in_ref, *refs):
    out_ref, sum_ref, expand_ref, squares_ref = refs[-4:]
    width = in_ref.shape[1]
    base = pl.multiple_of(width - at_ref[1] if second else at_ref[1], 128)
    expander(expand_ref, 5, base)
    blocks = [slice(c, c + BLOCK) for c in range(0, y_ref.shape[0], BLOCK)]
    for rows in blocks:
        c_block = c_ref[rows, :]
        q_short = q_ref[rows, :].astype(BF16)
        squares = None
        for part in tiles(width, 256):
            size = part.stop - part.start
            columns = pl.ds(pl.multiple_of(base + part.start, 128), size)
            grown = jnp.dot(q_short, expand_ref[:, part], preferred_element_type=F32)
            carried = jnp.dot(c_block, in_ref[:, part], preferred_element_type=F32)
            gated = (y_ref[rows, columns] + grown * carried) * silu(z_ref[rows, columns].astype(F32))
            out_ref[rows, columns] = gated
            square = gated * gated
            for i in range(0, size, 128):
                one = square[:, i : i + 128]
                squares = one if squares is None else squares + one
        squares_ref[rows, :] = squares
    for rows in blocks:
        total = jnp.sum(squares_ref[rows, :].T, axis=0, keepdims=True)
        sum_ref[:, rows] = refs[0][:, rows] + total if second else total


def gate(at, c_act, y, z, q, incoming, *before):
    length, width = y.shape
    return pl.pallas_call(
        functools.partial(gate_kernel, len(before) > 0),
        out_shape=[
            kept_in_vmem((length, width), F32),
            kept_in_vmem((1, length), F32),
        ],
        in_specs=[whole(pltpu.SMEM)] + [whole()] * (5 + len(before)),
        out_specs=[whole()] * 2,
        scratch_shapes=[
            pltpu.VMEM((128, incoming.shape[1]), BF16),
            pltpu.VMEM((length, 128), F32),
        ],
        input_output_aliases={2: 0},
        compiler_params=params(),
        cost_estimate=cost(0, 8 * length * width),
    )(at, c_act, y, z, q, incoming, *before)


def norm_kernel(g_ref, one_ref, two_ref, gain_ref, out_ref, held, sems):
    copies = []
    for c in range(g_ref.shape[0] // BLOCK):
        rows = slice(c * BLOCK, (c + 1) * BLOCK)
        square_sum = one_ref[:, rows] + two_ref[:, rows]
        inverse = lax.rsqrt(square_sum / INNER + 1e-05)
        scale = jnp.broadcast_to(inverse, (128, BLOCK)).T
        for i in range(0, g_ref.shape[1], 128):
            columns = slice(i, i + 128)
            held[c, :, columns] = (g_ref[rows, columns] * scale * gain_ref[:, columns]).astype(BF16)
        copy = pltpu.make_async_copy(held.at[c], out_ref.at[rows, :], sems.at[c])
        copy.start()
        copies.append(copy)
    for copy in copies:
        copy.wait()


def norm(gated, one, two, gain):
    length, width = gated.shape
    count = length // BLOCK
    return pl.pallas_call(
        norm_kernel,
        out_shape=jax.ShapeDtypeStruct((length, width), BF16),
        in_specs=[whole()] * 4,
        out_specs=whole(pltpu.HBM),
        scratch_shapes=[
            pltpu.VMEM((count, BLOCK, width), BF16),
            pltpu.SemaphoreType.DMA((count,)),
        ],
        compiler_params=params(),
        cost_estimate=cost(0, 0),
    )(gated, one, two, gain)


SWAP = [(0, 1), (1, 0), (2, 3), (3, 2)]


def zone_shift(a, k):
    size = lax.axis_size("head")
    return lax.ppermute(a, "head", [(i, (i + 2 * k) % size) for i in range(size)])


def side_swap(a):
    size = lax.axis_size("head")
    return lax.ppermute(a, "head", [(i, i ^ 1) for i in range(size)])


def chained_state(at, kept, sent, own, after, late):
    size = lax.axis_size("seq")
    if size == 4:
        got = [lax.ppermute(piece, "seq", SWAP) for piece in sent]
        both, got, partner = meet(at, kept, own, got, late)
        crossed = lax.ppermute(both, "seq", [(0, 2), (1, 3)])
        mine, passed = arrive(at, crossed, kept, got, own, partner, after)
        return mine, lax.ppermute(passed, "seq", SWAP)
    totals = lax.all_gather(jnp.concatenate([kept, *[a[:STATE] for a in sent]], axis=1), "seq")
    decays = lax.all_gather(own, "seq")

    def one(hop, state):
        decay = lax.dynamic_index_in_dim(decays, hop, 0, False)
        return decay * state + lax.dynamic_index_in_dim(totals, hop, 0, False).astype(F32)

    place = lax.axis_index("seq")
    state = lax.fori_loop(0, place, one, jnp.zeros(totals.shape[1:], F32)).astype(BF16)
    half = kept.shape[1]
    return state[:, :half], state[:, half:]


def on_device(x_inner, z_gate, bc_raw, conv_weight, conv_bias, dt_raw, a_log, d_skip, norm_gain):
    x_inner, z_gate = in_hbm(x_inner), in_hbm(z_gate)
    head_count = a_log.shape[0]
    own_rows = bc_raw.shape[0]
    seq_size = lax.axis_size("seq")
    shifts = range(1, lax.axis_size("head") // 2)
    width = x_inner.shape[1]
    first_channel = 0
    if seq_size == 4:
        first_channel = (1 - lax.rem(lax.axis_index("seq"), 2)) * (width // 2)
    place = jnp.stack([lax.axis_index("head"), first_channel]).astype(jnp.int32)
    own_b, own_c, place = prepare(place, bc_raw)
    zones_b = [zone_shift(own_b, k) for k in shifts]
    side_b = side_swap(own_b)
    pad = SLOT - head_count
    q, brow, dec, own_decay, xs_first, xs_later = rates(
        jnp.pad(dt_raw.T, ((0, pad), (0, 0))),
        jnp.pad(a_log, (0, pad))[None, :],
        jnp.pad(d_skip, (0, pad))[None, :],
        x_inner,
    )
    side_c = side_swap(own_c)
    cat_b, pair_c = pack(zones_b, own_c, side_c, xs_first, side_b)
    others_b = side_swap(cat_b)
    pairs_c = [zone_shift(pair_c, k) for k in shifts]
    per = own_b.shape[0]
    sources_b = [own_b, side_b, *zones_b, others_b]
    plan_b = [(0, 0, False, 0), (1, 0, True, 0)]
    plan_b += [(k + 1, 0, False, k) for k in shifts]
    plan_b += [(len(zones_b) + 2, (k - 1) * per, True, k) for k in shifts]
    sources_c = [pair_c, *pairs_c]
    plan_c = [(k, 0, False, k) for k in range(len(sources_c))]
    plan_c += [(k, own_rows, True, k) for k in range(len(sources_c))]
    bias = conv_bias[None, :]
    b_act, first_b, last_rows = activate(
        place, sources_b, plan_b, True, conv_weight, bias, own_rows, [xs_first]
    )
    rims = lax.ppermute(last_rows, "seq", [(i, i + 1) for i in range(seq_size - 1)])
    starts, later = later_states(b_act, xs_later, dec)
    b_act, state_0, kept, *sent = first_state(
        place, b_act, first_b, rims, conv_weight, bias, xs_first, dec, later, own_decay
    )
    c_act, _, _ = activate(place, [*sources_c, rims], plan_c, False, conv_weight, bias, own_rows)
    local, z_held = inner(c_act, b_act, x_inner, z_gate, q, brow, starts, state_0, dec)
    state_one, state_two = chained_state(place, kept, sent, own_decay, local, pairs_c)
    gated, square_one = gate(place, c_act, local, z_held, q, state_one)
    gated, square_sum = gate(place, c_act, gated, z_held, q, state_two, square_one)
    column = sum([zone_shift(square_sum, k) for k in shifts], square_sum)
    return norm(gated, column, side_swap(column), norm_gain[None, :])


def solution(mesh):
    placed = (
        P("seq", "head"),
        P("seq", "head"),
        P(("seq", "head"), None),
        P(),
        P(),
        P("seq", "head"),
        P("head"),
        P("head"),
        P("head"),
    )
    return jax.shard_map(
        on_device, mesh=mesh, in_specs=placed, out_specs=P("seq", "head"), check_vma=False
    )
```

```python
import functools
import math

import jax
import jax.numpy as jnp
from jax import lax
from jax.experimental import pallas as pl
from jax.experimental.pallas import tpu as pltpu
from jax.sharding import PartitionSpec as P

HEAD_DIM = 128
STATE = 256
BLOCK = 256
INNER = 16384
RIM = 16
SLOT = 16
PIECES = 4
LOG2E = math.log2(math.e)
F32 = jnp.float32
BF16 = jnp.bfloat16
HIGHEST = lax.Precision.HIGHEST
VMEM_LIMIT = 14 * 1024 * 1024


def params():
    return pltpu.CompilerParams(vmem_limit_bytes=VMEM_LIMIT)


def whole(memory_space=pltpu.VMEM):
    return pl.BlockSpec(memory_space=memory_space)


def kept_in_vmem(shape, dtype):
    return pltpu.VMEM(shape, dtype)


def stream_in(hbm_ref, held, sems, columns=None):
    copies = []
    for c in range(held.shape[0]):
        rows = pl.ds(c * BLOCK, BLOCK)
        source = hbm_ref.at[rows, :] if columns is None else hbm_ref.at[rows, columns]
        copy = pltpu.make_async_copy(source, held.at[c], sems.at[c])
        copy.start()
        copies.append(copy)
    return copies


def in_hbm(a):
    return pltpu.with_memory_space_constraint(a, pltpu.HBM)


def cost(flops, nbytes, trans=0):
    return pl.CostEstimate(flops=int(flops), bytes_accessed=int(nbytes), transcendentals=int(trans))


def silu(v):
    half = 0.5 * v
    return half + half * jnp.tanh(half)


def split(v):
    high = v.astype(BF16).astype(F32)
    return high, v - high


def conv_slab(slab, weight, bias):
    taps = weight.shape[0]
    total = jnp.broadcast_to(bias, slab.shape)
    for k in range(taps):
        shift = taps - 1 - k
        moved = pltpu.roll(slab, shift, 0) if shift else slab
        total = total + weight[k : k + 1, :] * moved
    total = total[RIM:]
    return (total * jax.nn.sigmoid(total)).astype(BF16)


def rates_kernel(
    dt_hbm, a_ref, skip_ref, x_ref, q_ref, b_ref, dec_ref, own_ref, first_ref, later_ref,
    dt_ref, expand_ref, held, sems, dt_sem,
):
    dt_copy = pltpu.make_async_copy(dt_hbm, dt_ref, dt_sem)
    dt_copy.start()
    copies = stream_in(x_ref, held, sems)
    expander(expand_ref, 1, 0)
    block_count = dt_ref.shape[1] // BLOCK
    diagonal = lax.broadcasted_iota(jnp.int32, (SLOT, SLOT), 0) == lax.broadcasted_iota(
        jnp.int32, (SLOT, SLOT), 1
    )

    def upright(row):
        return jnp.sum(jnp.where(diagonal, row, 0.0), axis=1, keepdims=True)

    rate = -jnp.exp(upright(a_ref[...]))
    upper = (
        lax.broadcasted_iota(jnp.int32, (BLOCK, BLOCK), 0)
        <= lax.broadcasted_iota(jnp.int32, (BLOCK, BLOCK), 1)
    ).astype(F32)
    prior = jnp.zeros((SLOT, 1), F32)
    later = jnp.zeros((SLOT, 1), F32)
    lane = lax.broadcasted_iota(jnp.int32, (SLOT, SLOT), 1)
    logs = jnp.zeros((SLOT, SLOT), F32)
    dt_copy.wait()
    for c in range(block_count):
        columns = slice(c * BLOCK, (c + 1) * BLOCK)
        dt = dt_ref[:, columns]
        step = jnp.maximum(dt, 0.0) + jnp.log1p(jnp.exp(-jnp.abs(dt)))
        cum = jnp.dot(rate * step, upper, precision=HIGHEST, preferred_element_type=F32)
        last = cum[:, BLOCK - 1 : BLOCK]
        scaled = cum * LOG2E
        b_ref[:, columns] = scaled - jnp.log(step) * LOG2E
        parts = [scaled]
        parts.extend(split(jnp.exp(last - cum) * step))
        parts.extend(split(jnp.exp(cum)))
        parts.extend(split(jnp.exp(cum + prior)))
        parts.append(jnp.zeros_like(cum))
        q_ref[columns, :] = jnp.concatenate(parts, axis=0).T
        logs = jnp.where(lane == c, last, logs)
        logs = jnp.where(lane == block_count + c, later, logs)
        prior = prior + last
        if c > 0:
            later = later + last
    logs = jnp.where(lane == 2 * block_count, later, logs)
    logs = jnp.where(lane == SLOT - 1, prior, logs)
    factors = jnp.where(lane == 2 * block_count + 1, upright(skip_ref[...]), jnp.exp(logs))
    width = dec_ref.shape[1]
    head = lax.broadcasted_iota(jnp.int32, (SLOT, width), 1) // HEAD_DIM
    spread = (lax.broadcasted_iota(jnp.int32, (SLOT, width), 0) == head).astype(F32)
    rows = lax.dot_general(
        factors, spread, (((0,), (0,)), ((), ())), precision=HIGHEST, preferred_element_type=F32
    )
    dec_ref[...] = rows
    own_ref[...] = rows[SLOT - 1 : SLOT]
    for copy in copies:
        copy.wait()
    for c in range(block_count):
        rows = slice(c * BLOCK, (c + 1) * BLOCK)
        q_block = q_ref[rows, :].astype(BF16)
        for columns in tiles(width):
            weight = jnp.dot(q_block, expand_ref[:, columns], preferred_element_type=F32)
            scaled = (held[c, :, columns].astype(F32) * weight).astype(BF16)
            if c == 0:
                first_ref[:, columns] = scaled
            else:
                later_ref[(c - 1) * BLOCK : c * BLOCK, columns] = scaled


def rates(dt, a_log, d_skip, x):
    length, width = x.shape
    count = length // BLOCK
    return pl.pallas_call(
        rates_kernel,
        out_shape=[
            kept_in_vmem((length, 128), F32),
            kept_in_vmem((SLOT, length), F32),
            kept_in_vmem((SLOT, width), F32),
            kept_in_vmem((1, width), F32),
            kept_in_vmem((BLOCK, width), BF16),
            kept_in_vmem((length - BLOCK, width), BF16),
        ],
        in_specs=[whole(pltpu.HBM), whole(), whole(), whole(pltpu.HBM)],
        out_specs=[whole()] * 6,
        scratch_shapes=[
            pltpu.VMEM(dt.shape, F32),
            pltpu.VMEM((128, width), BF16),
            pltpu.VMEM((count, BLOCK, width), BF16),
            pltpu.SemaphoreType.DMA((count,)),
            pltpu.SemaphoreType.DMA,
        ],
        compiler_params=params(),
        cost_estimate=cost(0, 0),
    )(in_hbm(dt), a_log, d_skip, x)


def expander(ref, slot, base):
    row = lax.broadcasted_iota(jnp.int32, ref.shape, 0)
    head = (lax.broadcasted_iota(jnp.int32, ref.shape, 1) + base) // HEAD_DIM
    ref[...] = ((row == slot * SLOT + head) | (row == (slot + 1) * SLOT + head)).astype(BF16)


def prepare_kernel(place_ref, bc_ref, b_ref, c_ref, place_out, sems):
    rows = bc_ref.shape[0]
    copies = [
        pltpu.make_async_copy(bc_ref.at[:, 0:STATE], b_ref.at[0:rows, :], sems.at[0]),
        pltpu.make_async_copy(
            bc_ref.at[rows - RIM : rows, STATE : 2 * STATE], b_ref.at[rows : rows + RIM, :], sems.at[1]
        ),
        pltpu.make_async_copy(bc_ref.at[:, STATE : 2 * STATE], c_ref, sems.at[2]),
    ]
    for copy in copies:
        copy.start()
    for i in range(place_ref.shape[0]):
        place_out[i] = place_ref[i]
    for copy in copies:
        copy.wait()


def prepare(place, bc_raw):
    rows = bc_raw.shape[0]
    return pl.pallas_call(
        prepare_kernel,
        out_shape=[
            jax.ShapeDtypeStruct((rows + RIM, STATE), BF16),
            jax.ShapeDtypeStruct((rows, STATE), BF16),
            pltpu.SMEM(place.shape, jnp.int32),
        ],
        in_specs=[whole(pltpu.SMEM), whole(pltpu.HBM)],
        out_specs=[whole(), whole(), whole(pltpu.SMEM)],
        scratch_shapes=[pltpu.SemaphoreType.DMA((3,))],
        compiler_params=params(),
        cost_estimate=cost(0, 0),
    )(place, in_hbm(bc_raw))


def pack_kernel(count, *refs):
    own_ref, side_ref = refs[count : count + 2]
    cat_ref, pair_ref = refs[-2:]
    per = refs[0].shape[0]
    for i in range(count):
        cat_ref[i * per : (i + 1) * per, :] = refs[i][...]
    rows = own_ref.shape[0]
    pair_ref[0:rows, :] = own_ref[...]
    pair_ref[rows : 2 * rows, :] = side_ref[...]


def pack(zones, own, side, *after):
    rows, columns = zones[0].shape
    return pl.pallas_call(
        functools.partial(pack_kernel, len(zones)),
        out_shape=[
            jax.ShapeDtypeStruct((len(zones) * rows, columns), BF16),
            jax.ShapeDtypeStruct((2 * own.shape[0], columns), BF16),
        ],
        in_specs=[whole()] * (len(zones) + 2) + [whole(pl.ANY)] * len(after),
        out_specs=[whole()] * 2,
        compiler_params=params(),
        cost_estimate=cost(0, 0),
    )(*zones, own, side, *after)


def act_kernel(own_rows, plan, is_b, me_ref, weight_ref, bias_ref, *refs):
    sources = refs[: 1 + max(index for index, *_ in plan) + (not is_b)]
    act_ref, first_ref, last_ref, raw = refs[-4:]
    me = me_ref[0]
    size = act_ref.shape[0] // own_rows
    partner = me + 1 - 2 * lax.rem(me, 2)
    if is_b:
        raw[0:RIM, :] = jnp.zeros((RIM, STATE), BF16)
    else:
        raw[0:RIM, :] = sources[-1][RIM : 2 * RIM, :]
    for index, start, side, shift in plan:
        ref = sources[index]
        owner = jnp.bitwise_xor(partner if side else me, 2 * shift)
        at = pl.multiple_of(RIM + owner * own_rows, 16)
        raw[pl.ds(at, own_rows), :] = ref[start : start + own_rows, :]
        if is_b:

            @pl.when(owner == size - 1)
            def _(ref=ref, start=start):
                end = start + own_rows
                last_ref[0:RIM, :] = ref[end - RIM : end, :]
                last_ref[RIM : 2 * RIM, :] = ref[end : end + RIM, :]

    first_ref[...] = raw[RIM : 2 * RIM, :]
    part = slice(0, STATE) if is_b else slice(STATE, 2 * STATE)
    weight = weight_ref[:, part]
    bias = bias_ref[:, part]
    for c in range(act_ref.shape[0] // BLOCK):
        slab = raw[c * BLOCK : c * BLOCK + RIM + BLOCK, :].astype(F32)
        act_ref[c * BLOCK : (c + 1) * BLOCK, :] = conv_slab(slab, weight, bias)


def activate(me, sources, plan, is_b, weight, bias, own_rows, after=()):
    length = len(plan) * own_rows
    return pl.pallas_call(
        functools.partial(act_kernel, own_rows, plan, is_b),
        out_shape=[
            kept_in_vmem((length, STATE), BF16),
            kept_in_vmem((RIM, STATE), BF16),
            kept_in_vmem((2 * RIM, STATE), BF16),
        ],
        in_specs=[whole(pltpu.SMEM)]
        + [whole()] * (len(sources) + 2)
        + [whole(pl.ANY)] * len(after),
        out_specs=[whole()] * 3,
        scratch_shapes=[pltpu.VMEM((RIM + length, STATE), BF16)],
        compiler_params=params(),
        cost_estimate=cost(0, 0),
    )(me, weight, bias, *sources, *after)


def tiles(width, step=512):
    step = min(step, width)
    return [slice(i, i + step) for i in range(0, width, step)]


def block_state(b_block, scaled):
    return lax.dot_general(
        b_block, scaled, (((0,), (0,)), ((), ())), preferred_element_type=F32
    )


def later_states_kernel(b_ref, xs_ref, dec_ref, *refs):
    starts_ref, total_ref = refs[-2:]
    for c in range(1, b_ref.shape[0] // BLOCK):
        rows = slice(c * BLOCK, (c + 1) * BLOCK)
        b_block = b_ref[rows, :]
        for columns in tiles(xs_ref.shape[1]):
            state = block_state(b_block, xs_ref[(c - 1) * BLOCK : c * BLOCK, columns])
            if c == 1:
                starts_ref[0, :, columns] = jnp.zeros_like(state).astype(BF16)
                total_ref[:, columns] = state
            else:
                before = total_ref[:, columns]
                starts_ref[c - 1, :, columns] = before.astype(BF16)
                total_ref[:, columns] = dec_ref[c : c + 1, columns] * before + state


def later_states(b_act, xs, dec, after=()):
    length, width = xs.shape
    return pl.pallas_call(
        later_states_kernel,
        out_shape=[
            kept_in_vmem((length // BLOCK, STATE, width), BF16),
            kept_in_vmem((STATE, width), F32),
        ],
        in_specs=[whole()] * 3 + [whole(pl.ANY)] * len(after),
        out_specs=[whole()] * 2,
        compiler_params=params(),
        cost_estimate=cost(0, 0),
    )(b_act, xs, dec, *after)


def first_state_kernel(
    at_ref, b_ref, first_ref, rim_ref, weight_ref, bias_ref, xs_ref, dec_ref, later_ref, *refs
):
    own_ref, b_out, state_ref, kept_ref, *sent_refs, total_ref = refs
    slab = jnp.concatenate([rim_ref[0:RIM, :], first_ref[...]], axis=0).astype(F32)
    fixed = conv_slab(slab, weight_ref[:, :STATE], bias_ref[:, :STATE])
    b_block = jnp.concatenate([fixed, b_ref[RIM:BLOCK, :]], axis=0)
    b_out[0:RIM, :] = fixed
    row = 2 * (b_out.shape[0] // BLOCK)
    for columns in tiles(xs_ref.shape[1]):
        state = block_state(b_block, xs_ref[0:BLOCK, columns])
        state_ref[:, columns] = state
        total = later_ref[:, columns] + dec_ref[row : row + 1, columns] * state
        total_ref[:, columns] = total.astype(BF16)
    half = kept_ref.shape[1]
    at = pl.multiple_of(at_ref[1], 128)
    kept_ref[...] = total_ref[:, pl.ds(at, half)]
    size = half // len(sent_refs)
    row_index = lax.broadcasted_iota(jnp.int32, (RIM, size), 0)
    for i, sent_ref in enumerate(sent_refs):
        columns = pl.ds(pl.multiple_of(half - at + i * size, 128), size)
        sent_ref[0:STATE, :] = total_ref[:, columns]
        rest = own_ref[:, columns]
        rows = jnp.zeros((RIM, size), F32)
        for k in range(3):
            term = rest.astype(BF16).astype(F32)
            rows = jnp.where(row_index == k, term, rows)
            rest = rest - term
        sent_ref[STATE : STATE + RIM, :] = rows.astype(BF16)


def first_state(at, b_act, first, rim, weight, bias, xs, dec, later, own):
    width = xs.shape[1]
    pieces = PIECES if width >= 256 * PIECES else 1
    return pl.pallas_call(
        first_state_kernel,
        out_shape=[
            kept_in_vmem(b_act.shape, BF16),
            kept_in_vmem((STATE, width), F32),
            kept_in_vmem((STATE, width // 2), BF16),
        ]
        + [kept_in_vmem((STATE + RIM, width // 2 // pieces), BF16)] * pieces,
        in_specs=[whole(pltpu.SMEM)] + [whole()] * 9,
        out_specs=[whole()] * (3 + pieces),
        scratch_shapes=[pltpu.VMEM((STATE, width), BF16)],
        input_output_aliases={1: 0},
        compiler_params=params(),
        cost_estimate=cost(0, 0),
    )(at, b_act, first, rim, weight, bias, xs, dec, later, own)


def meet_kernel(count, at_ref, kept_ref, own_ref, *refs):
    got_refs = refs[:count]
    out_ref, got_ref, partner_ref = refs[-3:]
    size = got_refs[0].shape[1]
    for i, ref in enumerate(got_refs):
        part = slice(i * size, (i + 1) * size)
        got_ref[:, part] = ref[0:STATE, :]
        rows = ref[STATE : STATE + RIM, :].astype(F32)
        partner_ref[:, part] = rows[0:1] + rows[1:2] + rows[2:3]
    half = kept_ref.shape[1]
    columns = pl.ds(pl.multiple_of(at_ref[1], 128), half)
    odd = at_ref[1] == 0
    kept_decay = jnp.where(odd, 1.0, partner_ref[...])
    got_decay = jnp.where(odd, own_ref[:, columns], 1.0)
    both = kept_decay * kept_ref[...].astype(F32) + got_decay * got_ref[...].astype(F32)
    out_ref[...] = both.astype(BF16)


def meet(at, kept, own, got, after):
    return pl.pallas_call(
        functools.partial(meet_kernel, len(got)),
        out_shape=[kept_in_vmem(kept.shape, BF16)] * 2
        + [kept_in_vmem((1, kept.shape[1]), F32)],
        in_specs=[whole(pltpu.SMEM)]
        + [whole()] * (2 + len(got))
        + [whole(pl.ANY)] * len(after),
        out_specs=[whole()] * 3,
        compiler_params=params(),
        cost_estimate=cost(0, 0),
    )(at, kept, own, *got, *after)


def arrive_kernel(at_ref, crossed_ref, kept_ref, got_ref, own_ref, partner_ref, *refs):
    in_ref, sent_ref = refs[-2:]
    half = kept_ref.shape[1]
    columns = pl.ds(pl.multiple_of(at_ref[1], 128), half)
    odd = at_ref[1] == 0
    decay = jnp.where(odd, partner_ref[...], own_ref[:, columns])
    crossed = crossed_ref[...]
    mine = jnp.where(odd, got_ref[...].astype(F32), kept_ref[...].astype(F32))
    after_even = (decay * crossed.astype(F32) + mine).astype(BF16)
    in_ref[...] = jnp.where(odd, after_even, crossed)
    sent_ref[...] = jnp.where(odd, crossed, after_even)


def arrive(at, crossed, kept, got, own, partner, after):
    return pl.pallas_call(
        arrive_kernel,
        out_shape=[kept_in_vmem(kept.shape, BF16)] * 2,
        in_specs=[whole(pltpu.SMEM)] + [whole()] * 5 + [whole(pl.ANY)],
        out_specs=[whole()] * 2,
        compiler_params=params(),
        cost_estimate=cost(0, 0),
    )(at, crossed, kept, got, own, partner, after)


def inner_kernel(
    c_ref, b_ref, x_ref, z_ref, q_ref, brow_ref, starts_ref, state_ref, dec_ref,
    out_ref, z_out, expand_ref, held, sems, z_sem,
):
    copies = stream_in(x_ref, held, sems)
    z_copy = pltpu.make_async_copy(z_ref, z_out, z_sem)
    z_copy.start()
    half = BLOCK // 2
    block_count = x_ref.shape[0] // BLOCK
    head_count = x_ref.shape[1] // HEAD_DIM
    expander(expand_ref, 3, 0)
    lower = lax.broadcasted_iota(jnp.int32, (half, half), 0) >= lax.broadcasted_iota(
        jnp.int32, (half, half), 1
    )

    for c in range(block_count):
        rows = slice(c * BLOCK, (c + 1) * BLOCK)
        c_block = c_ref[rows, :]
        q_block = q_ref[rows, :]
        if c > 0:
            q_short = q_block.astype(BF16)
            for columns in tiles(x_ref.shape[1], 256):
                decay = dec_ref[block_count + c : block_count + c + 1, columns]
                start = starts_ref[c - 1, :, columns].astype(F32) + decay * state_ref[:, columns]
                grown = jnp.dot(q_short, expand_ref[:, columns], preferred_element_type=F32)
                carried = jnp.dot(c_block, start.astype(BF16), preferred_element_type=F32)
                out_ref[rows, columns] = grown * carried
        copies[c].wait()
        gram = lax.dot_general(
            c_block, b_ref[rows, :], (((1,), (1,)), ((), ())), preferred_element_type=F32
        )
        gram_00 = jnp.where(lower, gram[:half, :half], 0.0)
        gram_10 = gram[half:, :half]
        gram_11 = jnp.where(lower, gram[half:, half:], 0.0)
        for h in range(head_count):
            columns = slice(h * HEAD_DIM, (h + 1) * HEAD_DIM)
            rise = jnp.broadcast_to(q_block[:, h : h + 1], (BLOCK, half))
            fall = brow_ref[h : h + 1, rows]
            w_00 = gram_00 * jnp.exp2(jnp.minimum(rise[:half] - fall[:, :half], 120.0))
            w_10 = gram_10 * jnp.exp2(rise[half:] - fall[:, :half])
            w_11 = gram_11 * jnp.exp2(jnp.minimum(rise[half:] - fall[:, half:], 120.0))
            x_head = held[c, :, columns]
            top = jnp.dot(w_00.astype(BF16), x_head[:half], preferred_element_type=F32)
            low = jnp.concatenate([w_10.astype(BF16), w_11.astype(BF16)], axis=1)
            bottom = jnp.dot(low, x_head, preferred_element_type=F32)
            skip = dec_ref[2 * block_count + 1 : 2 * block_count + 2, columns] * x_head.astype(F32)
            own = jnp.concatenate([top, bottom], axis=0) + skip
            if c > 0:
                own = own + out_ref[rows, columns]
            out_ref[rows, columns] = own

    z_copy.wait()


def inner(c_act, b_act, x, z, q, brow, starts, state, dec):
    length, width = x.shape
    return pl.pallas_call(
        inner_kernel,
        out_shape=[kept_in_vmem((length, width), F32), kept_in_vmem(z.shape, z.dtype)],
        in_specs=[whole()] * 2 + [whole(pltpu.HBM)] * 2 + [whole()] * 5,
        out_specs=[whole()] * 2,
        scratch_shapes=[
            pltpu.VMEM((128, width), BF16),
            pltpu.VMEM((length // BLOCK, BLOCK, width), BF16),
            pltpu.SemaphoreType.DMA((length // BLOCK,)),
            pltpu.SemaphoreType.DMA,
        ],
        compiler_params=params(),
        cost_estimate=cost(0, 80 * length * width),
    )(c_act, b_act, x, z, q, brow, starts, state, dec)


def gate_kernel(second, at_ref, c_ref, y_ref, z_ref, q_ref, in_ref, *refs):
    out_ref, sum_ref, expand_ref, squares_ref = refs[-4:]
    width = in_ref.shape[1]
    base = pl.multiple_of(width - at_ref[1] if second else at_ref[1], 128)
    expander(expand_ref, 5, base)
    blocks = [slice(c, c + BLOCK) for c in range(0, y_ref.shape[0], BLOCK)]
    for rows in blocks:
        c_block = c_ref[rows, :]
        q_short = q_ref[rows, :].astype(BF16)
        squares = None
        for part in tiles(width, 256):
            size = part.stop - part.start
            columns = pl.ds(pl.multiple_of(base + part.start, 128), size)
            grown = jnp.dot(q_short, expand_ref[:, part], preferred_element_type=F32)
            carried = jnp.dot(c_block, in_ref[:, part], preferred_element_type=F32)
            gated = (y_ref[rows, columns] + grown * carried) * silu(z_ref[rows, columns].astype(F32))
            out_ref[rows, columns] = gated
            square = gated * gated
            for i in range(0, size, 128):
                one = square[:, i : i + 128]
                squares = one if squares is None else squares + one
        squares_ref[rows, :] = squares
    for rows in blocks:
        total = jnp.sum(squares_ref[rows, :].T, axis=0, keepdims=True)
        sum_ref[:, rows] = refs[0][:, rows] + total if second else total


def gate(at, c_act, y, z, q, incoming, *before):
    length, width = y.shape
    return pl.pallas_call(
        functools.partial(gate_kernel, len(before) > 0),
        out_shape=[
            kept_in_vmem((length, width), F32),
            kept_in_vmem((1, length), F32),
        ],
        in_specs=[whole(pltpu.SMEM)] + [whole()] * (5 + len(before)),
        out_specs=[whole()] * 2,
        scratch_shapes=[
            pltpu.VMEM((128, incoming.shape[1]), BF16),
            pltpu.VMEM((length, 128), F32),
        ],
        input_output_aliases={2: 0},
        compiler_params=params(),
        cost_estimate=cost(0, 8 * length * width),
    )(at, c_act, y, z, q, incoming, *before)


def norm_kernel(g_ref, one_ref, two_ref, gain_ref, out_ref, held, sems):
    copies = []
    for c in range(g_ref.shape[0] // BLOCK):
        rows = slice(c * BLOCK, (c + 1) * BLOCK)
        square_sum = one_ref[:, rows] + two_ref[:, rows]
        inverse = lax.rsqrt(square_sum / INNER + 1e-05)
        scale = jnp.broadcast_to(inverse, (128, BLOCK)).T
        for i in range(0, g_ref.shape[1], 128):
            columns = slice(i, i + 128)
            held[c, :, columns] = (g_ref[rows, columns] * scale * gain_ref[:, columns]).astype(BF16)
        copy = pltpu.make_async_copy(held.at[c], out_ref.at[rows, :], sems.at[c])
        copy.start()
        copies.append(copy)
    for copy in copies:
        copy.wait()


def norm(gated, one, two, gain):
    length, width = gated.shape
    count = length // BLOCK
    return pl.pallas_call(
        norm_kernel,
        out_shape=jax.ShapeDtypeStruct((length, width), BF16),
        in_specs=[whole()] * 4,
        out_specs=whole(pltpu.HBM),
        scratch_shapes=[
            pltpu.VMEM((count, BLOCK, width), BF16),
            pltpu.SemaphoreType.DMA((count,)),
        ],
        compiler_params=params(),
        cost_estimate=cost(0, 0),
    )(gated, one, two, gain)


SWAP = [(0, 1), (1, 0), (2, 3), (3, 2)]


def zone_swap(a, k):
    size = lax.axis_size("head")
    return lax.ppermute(a, "head", [(i, i ^ (2 * k)) for i in range(size)])


def side_swap(a):
    size = lax.axis_size("head")
    return lax.ppermute(a, "head", [(i, i ^ 1) for i in range(size)])


def chained_state(at, kept, sent, own, after, late):
    size = lax.axis_size("seq")
    if size == 4:
        got = [lax.ppermute(piece, "seq", SWAP) for piece in sent]
        both, got, partner = meet(at, kept, own, got, late)
        crossed = lax.ppermute(both, "seq", [(0, 2), (1, 3)])
        mine, passed = arrive(at, crossed, kept, got, own, partner, after)
        return mine, lax.ppermute(passed, "seq", SWAP)
    totals = lax.all_gather(jnp.concatenate([kept, *[a[:STATE] for a in sent]], axis=1), "seq")
    decays = lax.all_gather(own, "seq")

    def one(hop, state):
        decay = lax.dynamic_index_in_dim(decays, hop, 0, False)
        return decay * state + lax.dynamic_index_in_dim(totals, hop, 0, False).astype(F32)

    place = lax.axis_index("seq")
    state = lax.fori_loop(0, place, one, jnp.zeros(totals.shape[1:], F32)).astype(BF16)
    half = kept.shape[1]
    return state[:, :half], state[:, half:]


def on_device(x_inner, z_gate, bc_raw, conv_weight, conv_bias, dt_raw, a_log, d_skip, norm_gain):
    x_inner, z_gate = in_hbm(x_inner), in_hbm(z_gate)
    head_count = a_log.shape[0]
    own_rows = bc_raw.shape[0]
    seq_size = lax.axis_size("seq")
    shifts = range(1, lax.axis_size("head") // 2)
    width = x_inner.shape[1]
    first_channel = 0
    if seq_size == 4:
        first_channel = (1 - lax.rem(lax.axis_index("seq"), 2)) * (width // 2)
    place = jnp.stack([lax.axis_index("head"), first_channel]).astype(jnp.int32)
    own_b, own_c, place = prepare(place, bc_raw)
    zones_b = [zone_swap(own_b, k) for k in shifts]
    side_b = side_swap(own_b)
    pad = SLOT - head_count
    q, brow, dec, own_decay, xs_first, xs_later = rates(
        jnp.pad(dt_raw.T, ((0, pad), (0, 0))),
        jnp.pad(a_log, (0, pad))[None, :],
        jnp.pad(d_skip, (0, pad))[None, :],
        x_inner,
    )
    side_c = side_swap(own_c)
    cat_b, pair_c = pack(zones_b, own_c, side_c, xs_first, side_b)
    others_b = side_swap(cat_b)
    pairs_c = [zone_swap(pair_c, k) for k in shifts]
    per = own_b.shape[0]
    sources_b = [own_b, side_b, *zones_b, others_b]
    plan_b = [(0, 0, False, 0), (1, 0, True, 0)]
    plan_b += [(k + 1, 0, False, k) for k in shifts]
    plan_b += [(len(zones_b) + 2, (k - 1) * per, True, k) for k in shifts]
    sources_c = [pair_c, *pairs_c]
    plan_c = [(k, 0, False, k) for k in range(len(sources_c))]
    plan_c += [(k, own_rows, True, k) for k in range(len(sources_c))]
    bias = conv_bias[None, :]
    b_act, first_b, last_rows = activate(
        place, sources_b, plan_b, True, conv_weight, bias, own_rows, [xs_first]
    )
    rims = lax.ppermute(last_rows, "seq", [(i, i + 1) for i in range(seq_size - 1)])
    starts, later = later_states(b_act, xs_later, dec)
    b_act, state_0, kept, *sent = first_state(
        place, b_act, first_b, rims, conv_weight, bias, xs_first, dec, later, own_decay
    )
    c_act, _, _ = activate(place, [*sources_c, rims], plan_c, False, conv_weight, bias, own_rows)
    local, z_held = inner(c_act, b_act, x_inner, z_gate, q, brow, starts, state_0, dec)
    state_one, state_two = chained_state(place, kept, sent, own_decay, local, pairs_c)
    gated, square_one = gate(place, c_act, local, z_held, q, state_one)
    gated, square_sum = gate(place, c_act, gated, z_held, q, state_two, square_one)
    column = sum([zone_swap(square_sum, k) for k in shifts], square_sum)
    return norm(gated, column, side_swap(column), norm_gain[None, :])


def solution(mesh):
    placed = (
        P("seq", "head"),
        P("seq", "head"),
        P(("seq", "head"), None),
        P(),
        P(),
        P("seq", "head"),
        P("head"),
        P("head"),
        P("head"),
    )
    return jax.shard_map(
        on_device, mesh=mesh, in_specs=placed, out_specs=P("seq", "head"), check_vma=False
    )
```

```python
import functools
import math

import jax
import jax.numpy as jnp
from jax import lax
from jax.experimental import pallas as pl
from jax.experimental.pallas import tpu as pltpu
from jax.sharding import PartitionSpec as P

HEAD_DIM = 128
STATE = 256
BLOCK = 256
INNER = 16384
RIM = 16
SLOT = 16
PIECES = 4
LOG2E = math.log2(math.e)
F32 = jnp.float32
BF16 = jnp.bfloat16
HIGHEST = lax.Precision.HIGHEST
VMEM_LIMIT = 14 * 1024 * 1024


def params():
    return pltpu.CompilerParams(vmem_limit_bytes=VMEM_LIMIT)


def whole(memory_space=pltpu.VMEM):
    return pl.BlockSpec(memory_space=memory_space)


def kept_in_vmem(shape, dtype):
    return pltpu.VMEM(shape, dtype)


def stream_in(hbm_ref, held, sems, columns=None):
    copies = []
    for c in range(held.shape[0]):
        rows = pl.ds(c * BLOCK, BLOCK)
        source = hbm_ref.at[rows, :] if columns is None else hbm_ref.at[rows, columns]
        copy = pltpu.make_async_copy(source, held.at[c], sems.at[c])
        copy.start()
        copies.append(copy)
    return copies


def in_hbm(a):
    return pltpu.with_memory_space_constraint(a, pltpu.HBM)


def cost(flops, nbytes, trans=0):
    return pl.CostEstimate(flops=int(flops), bytes_accessed=int(nbytes), transcendentals=int(trans))


def silu(v):
    half = 0.5 * v
    return half + half * jnp.tanh(half)


def split(v):
    high = v.astype(BF16).astype(F32)
    return high, v - high


def conv_slab(slab, weight, bias):
    taps = weight.shape[0]
    total = jnp.broadcast_to(bias, slab.shape)
    for k in range(taps):
        shift = taps - 1 - k
        moved = pltpu.roll(slab, shift, 0) if shift else slab
        total = total + weight[k : k + 1, :] * moved
    total = total[RIM:]
    return (total * jax.nn.sigmoid(total)).astype(BF16)


def rates_kernel(
    dt_hbm, a_ref, skip_ref, x_ref, q_ref, b_ref, dec_ref, own_ref, first_ref, later_ref,
    dt_ref, expand_ref, held, sems, dt_sem,
):
    dt_copy = pltpu.make_async_copy(dt_hbm, dt_ref, dt_sem)
    dt_copy.start()
    copies = stream_in(x_ref, held, sems)
    expander(expand_ref, 1, 0)
    block_count = dt_ref.shape[1] // BLOCK
    diagonal = lax.broadcasted_iota(jnp.int32, (SLOT, SLOT), 0) == lax.broadcasted_iota(
        jnp.int32, (SLOT, SLOT), 1
    )

    def upright(row):
        return jnp.sum(jnp.where(diagonal, row, 0.0), axis=1, keepdims=True)

    rate = -jnp.exp(upright(a_ref[...]))
    upper = (
        lax.broadcasted_iota(jnp.int32, (BLOCK, BLOCK), 0)
        <= lax.broadcasted_iota(jnp.int32, (BLOCK, BLOCK), 1)
    ).astype(F32)
    prior = jnp.zeros((SLOT, 1), F32)
    later = jnp.zeros((SLOT, 1), F32)
    lane = lax.broadcasted_iota(jnp.int32, (SLOT, SLOT), 1)
    logs = jnp.zeros((SLOT, SLOT), F32)
    dt_copy.wait()
    for c in range(block_count):
        columns = slice(c * BLOCK, (c + 1) * BLOCK)
        dt = dt_ref[:, columns]
        step = jnp.maximum(dt, 0.0) + jnp.log1p(jnp.exp(-jnp.abs(dt)))
        cum = jnp.dot(rate * step, upper, precision=HIGHEST, preferred_element_type=F32)
        last = cum[:, BLOCK - 1 : BLOCK]
        scaled = cum * LOG2E
        b_ref[0:SLOT, columns] = scaled
        b_ref[SLOT : 2 * SLOT, columns] = step
        parts = [scaled]
        parts.extend(split(jnp.exp(last - cum) * step))
        parts.extend(split(jnp.exp(cum)))
        parts.extend(split(jnp.exp(cum + prior)))
        parts.append(jnp.zeros_like(cum))
        q_ref[columns, :] = jnp.concatenate(parts, axis=0).T
        logs = jnp.where(lane == c, last, logs)
        logs = jnp.where(lane == block_count + c, later, logs)
        prior = prior + last
        if c > 0:
            later = later + last
    logs = jnp.where(lane == 2 * block_count, later, logs)
    logs = jnp.where(lane == SLOT - 1, prior, logs)
    factors = jnp.where(lane == 2 * block_count + 1, upright(skip_ref[...]), jnp.exp(logs))
    width = dec_ref.shape[1]
    head = lax.broadcasted_iota(jnp.int32, (SLOT, width), 1) // HEAD_DIM
    spread = (lax.broadcasted_iota(jnp.int32, (SLOT, width), 0) == head).astype(F32)
    rows = lax.dot_general(
        factors, spread, (((0,), (0,)), ((), ())), precision=HIGHEST, preferred_element_type=F32
    )
    dec_ref[...] = rows
    own_ref[...] = rows[SLOT - 1 : SLOT]
    for copy in copies:
        copy.wait()
    for c in range(block_count):
        rows = slice(c * BLOCK, (c + 1) * BLOCK)
        q_block = q_ref[rows, :].astype(BF16)
        for columns in tiles(width):
            weight = jnp.dot(q_block, expand_ref[:, columns], preferred_element_type=F32)
            scaled = (held[c, :, columns].astype(F32) * weight).astype(BF16)
            if c == 0:
                first_ref[:, columns] = scaled
            else:
                later_ref[(c - 1) * BLOCK : c * BLOCK, columns] = scaled


def rates(dt, a_log, d_skip, x):
    length, width = x.shape
    count = length // BLOCK
    return pl.pallas_call(
        rates_kernel,
        out_shape=[
            kept_in_vmem((length, 128), F32),
            kept_in_vmem((2 * SLOT, length), F32),
            kept_in_vmem((SLOT, width), F32),
            kept_in_vmem((1, width), F32),
            kept_in_vmem((BLOCK, width), BF16),
            kept_in_vmem((length - BLOCK, width), BF16),
        ],
        in_specs=[whole(pltpu.HBM), whole(), whole(), whole(pltpu.HBM)],
        out_specs=[whole()] * 6,
        scratch_shapes=[
            pltpu.VMEM(dt.shape, F32),
            pltpu.VMEM((128, width), BF16),
            pltpu.VMEM((count, BLOCK, width), BF16),
            pltpu.SemaphoreType.DMA((count,)),
            pltpu.SemaphoreType.DMA,
        ],
        compiler_params=params(),
        cost_estimate=cost(0, 0),
    )(in_hbm(dt), a_log, d_skip, x)


def expander(ref, slot, base):
    row = lax.broadcasted_iota(jnp.int32, ref.shape, 0)
    head = (lax.broadcasted_iota(jnp.int32, ref.shape, 1) + base) // HEAD_DIM
    ref[...] = ((row == slot * SLOT + head) | (row == (slot + 1) * SLOT + head)).astype(BF16)


def prepare_kernel(place_ref, bc_ref, b_ref, c_ref, place_out, sems):
    rows = bc_ref.shape[0]
    copies = [
        pltpu.make_async_copy(bc_ref.at[:, 0:STATE], b_ref.at[0:rows, :], sems.at[0]),
        pltpu.make_async_copy(
            bc_ref.at[rows - RIM : rows, STATE : 2 * STATE], b_ref.at[rows : rows + RIM, :], sems.at[1]
        ),
        pltpu.make_async_copy(bc_ref.at[:, STATE : 2 * STATE], c_ref, sems.at[2]),
    ]
    for copy in copies:
        copy.start()
    for i in range(place_ref.shape[0]):
        place_out[i] = place_ref[i]
    for copy in copies:
        copy.wait()


def prepare(place, bc_raw):
    rows = bc_raw.shape[0]
    return pl.pallas_call(
        prepare_kernel,
        out_shape=[
            jax.ShapeDtypeStruct((rows + RIM, STATE), BF16),
            jax.ShapeDtypeStruct((rows, STATE), BF16),
            pltpu.SMEM(place.shape, jnp.int32),
        ],
        in_specs=[whole(pltpu.SMEM), whole(pltpu.HBM)],
        out_specs=[whole(), whole(), whole(pltpu.SMEM)],
        scratch_shapes=[pltpu.SemaphoreType.DMA((3,))],
        compiler_params=params(),
        cost_estimate=cost(0, 0),
    )(place, in_hbm(bc_raw))


def pack_kernel(count, *refs):
    own_ref, side_ref = refs[count : count + 2]
    cat_ref, pair_ref = refs[-2:]
    per = refs[0].shape[0]
    for i in range(count):
        cat_ref[i * per : (i + 1) * per, :] = refs[i][...]
    rows = own_ref.shape[0]
    pair_ref[0:rows, :] = own_ref[...]
    pair_ref[rows : 2 * rows, :] = side_ref[...]


def pack(zones, own, side, *after):
    rows, columns = zones[0].shape
    return pl.pallas_call(
        functools.partial(pack_kernel, len(zones)),
        out_shape=[
            jax.ShapeDtypeStruct((len(zones) * rows, columns), BF16),
            jax.ShapeDtypeStruct((2 * own.shape[0], columns), BF16),
        ],
        in_specs=[whole()] * (len(zones) + 2) + [whole(pl.ANY)] * len(after),
        out_specs=[whole()] * 2,
        compiler_params=params(),
        cost_estimate=cost(0, 0),
    )(*zones, own, side, *after)


def act_kernel(own_rows, plan, is_b, me_ref, weight_ref, bias_ref, *refs):
    sources = refs[: 1 + max(index for index, *_ in plan) + (not is_b)]
    act_ref, first_ref, last_ref, raw = refs[-4:]
    me = me_ref[0]
    size = act_ref.shape[0] // own_rows
    partner = me + 1 - 2 * lax.rem(me, 2)
    if is_b:
        raw[0:RIM, :] = jnp.zeros((RIM, STATE), BF16)
    else:
        raw[0:RIM, :] = sources[-1][RIM : 2 * RIM, :]
    for index, start, side, shift in plan:
        ref = sources[index]
        owner = jnp.bitwise_xor(partner if side else me, 2 * shift)
        at = pl.multiple_of(RIM + owner * own_rows, 16)
        raw[pl.ds(at, own_rows), :] = ref[start : start + own_rows, :]
        if is_b:

            @pl.when(owner == size - 1)
            def _(ref=ref, start=start):
                end = start + own_rows
                last_ref[0:RIM, :] = ref[end - RIM : end, :]
                last_ref[RIM : 2 * RIM, :] = ref[end : end + RIM, :]

    first_ref[...] = raw[RIM : 2 * RIM, :]
    part = slice(0, STATE) if is_b else slice(STATE, 2 * STATE)
    weight = weight_ref[:, part]
    bias = bias_ref[:, part]
    for c in range(act_ref.shape[0] // BLOCK):
        slab = raw[c * BLOCK : c * BLOCK + RIM + BLOCK, :].astype(F32)
        act_ref[c * BLOCK : (c + 1) * BLOCK, :] = conv_slab(slab, weight, bias)


def activate(me, sources, plan, is_b, weight, bias, own_rows, after=()):
    length = len(plan) * own_rows
    return pl.pallas_call(
        functools.partial(act_kernel, own_rows, plan, is_b),
        out_shape=[
            kept_in_vmem((length, STATE), BF16),
            kept_in_vmem((RIM, STATE), BF16),
            kept_in_vmem((2 * RIM, STATE), BF16),
        ],
        in_specs=[whole(pltpu.SMEM)]
        + [whole()] * (len(sources) + 2)
        + [whole(pl.ANY)] * len(after),
        out_specs=[whole()] * 3,
        scratch_shapes=[pltpu.VMEM((RIM + length, STATE), BF16)],
        compiler_params=params(),
        cost_estimate=cost(0, 0),
    )(me, weight, bias, *sources, *after)


def tiles(width, step=512):
    step = min(step, width)
    return [slice(i, i + step) for i in range(0, width, step)]


def block_state(b_block, scaled):
    return lax.dot_general(
        b_block, scaled, (((0,), (0,)), ((), ())), preferred_element_type=F32
    )


def later_states_kernel(b_ref, xs_ref, dec_ref, *refs):
    starts_ref, total_ref = refs[-2:]
    for c in range(1, b_ref.shape[0] // BLOCK):
        rows = slice(c * BLOCK, (c + 1) * BLOCK)
        b_block = b_ref[rows, :]
        for columns in tiles(xs_ref.shape[1]):
            state = block_state(b_block, xs_ref[(c - 1) * BLOCK : c * BLOCK, columns])
            if c == 1:
                starts_ref[0, :, columns] = jnp.zeros_like(state).astype(BF16)
                total_ref[:, columns] = state
            else:
                before = total_ref[:, columns]
                starts_ref[c - 1, :, columns] = before.astype(BF16)
                total_ref[:, columns] = dec_ref[c : c + 1, columns] * before + state


def later_states(b_act, xs, dec, after=()):
    length, width = xs.shape
    return pl.pallas_call(
        later_states_kernel,
        out_shape=[
            kept_in_vmem((length // BLOCK, STATE, width), BF16),
            kept_in_vmem((STATE, width), F32),
        ],
        in_specs=[whole()] * 3 + [whole(pl.ANY)] * len(after),
        out_specs=[whole()] * 2,
        compiler_params=params(),
        cost_estimate=cost(0, 0),
    )(b_act, xs, dec, *after)


def first_state_kernel(
    at_ref, b_ref, first_ref, rim_ref, weight_ref, bias_ref, xs_ref, dec_ref, later_ref, *refs
):
    own_ref, b_out, state_ref, kept_ref, *sent_refs, total_ref = refs
    slab = jnp.concatenate([rim_ref[0:RIM, :], first_ref[...]], axis=0).astype(F32)
    fixed = conv_slab(slab, weight_ref[:, :STATE], bias_ref[:, :STATE])
    b_block = jnp.concatenate([fixed, b_ref[RIM:BLOCK, :]], axis=0)
    b_out[0:RIM, :] = fixed
    row = 2 * (b_out.shape[0] // BLOCK)
    for columns in tiles(xs_ref.shape[1]):
        state = block_state(b_block, xs_ref[0:BLOCK, columns])
        state_ref[:, columns] = state
        total = later_ref[:, columns] + dec_ref[row : row + 1, columns] * state
        total_ref[:, columns] = total.astype(BF16)
    half = kept_ref.shape[1]
    at = pl.multiple_of(at_ref[1], 128)
    kept_ref[...] = total_ref[:, pl.ds(at, half)]
    size = half // len(sent_refs)
    row_index = lax.broadcasted_iota(jnp.int32, (RIM, size), 0)
    for i, sent_ref in enumerate(sent_refs):
        columns = pl.ds(pl.multiple_of(half - at + i * size, 128), size)
        sent_ref[0:STATE, :] = total_ref[:, columns]
        rest = own_ref[:, columns]
        rows = jnp.zeros((RIM, size), F32)
        for k in range(3):
            term = rest.astype(BF16).astype(F32)
            rows = jnp.where(row_index == k, term, rows)
            rest = rest - term
        sent_ref[STATE : STATE + RIM, :] = rows.astype(BF16)


def first_state(at, b_act, first, rim, weight, bias, xs, dec, later, own):
    width = xs.shape[1]
    pieces = PIECES if width >= 256 * PIECES else 1
    return pl.pallas_call(
        first_state_kernel,
        out_shape=[
            kept_in_vmem(b_act.shape, BF16),
            kept_in_vmem((STATE, width), F32),
            kept_in_vmem((STATE, width // 2), BF16),
        ]
        + [kept_in_vmem((STATE + RIM, width // 2 // pieces), BF16)] * pieces,
        in_specs=[whole(pltpu.SMEM)] + [whole()] * 9,
        out_specs=[whole()] * (3 + pieces),
        scratch_shapes=[pltpu.VMEM((STATE, width), BF16)],
        input_output_aliases={1: 0},
        compiler_params=params(),
        cost_estimate=cost(0, 0),
    )(at, b_act, first, rim, weight, bias, xs, dec, later, own)


def meet_kernel(count, at_ref, kept_ref, own_ref, *refs):
    got_refs = refs[:count]
    out_ref, got_ref, partner_ref = refs[-3:]
    size = got_refs[0].shape[1]
    for i, ref in enumerate(got_refs):
        part = slice(i * size, (i + 1) * size)
        got_ref[:, part] = ref[0:STATE, :]
        rows = ref[STATE : STATE + RIM, :].astype(F32)
        partner_ref[:, part] = rows[0:1] + rows[1:2] + rows[2:3]
    half = kept_ref.shape[1]
    columns = pl.ds(pl.multiple_of(at_ref[1], 128), half)
    odd = at_ref[1] == 0
    kept_decay = jnp.where(odd, 1.0, partner_ref[...])
    got_decay = jnp.where(odd, own_ref[:, columns], 1.0)
    both = kept_decay * kept_ref[...].astype(F32) + got_decay * got_ref[...].astype(F32)
    out_ref[...] = both.astype(BF16)


def meet(at, kept, own, got, after):
    return pl.pallas_call(
        functools.partial(meet_kernel, len(got)),
        out_shape=[kept_in_vmem(kept.shape, BF16)] * 2
        + [kept_in_vmem((1, kept.shape[1]), F32)],
        in_specs=[whole(pltpu.SMEM)]
        + [whole()] * (2 + len(got))
        + [whole(pl.ANY)] * len(after),
        out_specs=[whole()] * 3,
        compiler_params=params(),
        cost_estimate=cost(0, 0),
    )(at, kept, own, *got, *after)


def arrive_kernel(at_ref, crossed_ref, kept_ref, got_ref, own_ref, partner_ref, *refs):
    in_ref, sent_ref = refs[-2:]
    half = kept_ref.shape[1]
    columns = pl.ds(pl.multiple_of(at_ref[1], 128), half)
    odd = at_ref[1] == 0
    decay = jnp.where(odd, partner_ref[...], own_ref[:, columns])
    crossed = crossed_ref[...]
    mine = jnp.where(odd, got_ref[...].astype(F32), kept_ref[...].astype(F32))
    after_even = (decay * crossed.astype(F32) + mine).astype(BF16)
    in_ref[...] = jnp.where(odd, after_even, crossed)
    sent_ref[...] = jnp.where(odd, crossed, after_even)


def arrive(at, crossed, kept, got, own, partner, after):
    return pl.pallas_call(
        arrive_kernel,
        out_shape=[kept_in_vmem(kept.shape, BF16)] * 2,
        in_specs=[whole(pltpu.SMEM)] + [whole()] * 5 + [whole(pl.ANY)],
        out_specs=[whole()] * 2,
        compiler_params=params(),
        cost_estimate=cost(0, 0),
    )(at, crossed, kept, got, own, partner, after)


def inner_kernel(
    c_ref, b_ref, x_ref, z_ref, q_ref, brow_ref, starts_ref, state_ref, dec_ref,
    out_ref, z_out, expand_ref, held, sems, z_sem,
):
    copies = stream_in(x_ref, held, sems)
    z_copy = pltpu.make_async_copy(z_ref, z_out, z_sem)
    z_copy.start()
    half = BLOCK // 2
    block_count = x_ref.shape[0] // BLOCK
    head_count = x_ref.shape[1] // HEAD_DIM
    expander(expand_ref, 3, 0)
    lower = lax.broadcasted_iota(jnp.int32, (half, half), 0) >= lax.broadcasted_iota(
        jnp.int32, (half, half), 1
    )

    for c in range(block_count):
        rows = slice(c * BLOCK, (c + 1) * BLOCK)
        c_block = c_ref[rows, :]
        q_block = q_ref[rows, :]
        if c > 0:
            q_short = q_block.astype(BF16)
            for columns in tiles(x_ref.shape[1], 256):
                decay = dec_ref[block_count + c : block_count + c + 1, columns]
                start = starts_ref[c - 1, :, columns].astype(F32) + decay * state_ref[:, columns]
                grown = jnp.dot(q_short, expand_ref[:, columns], preferred_element_type=F32)
                carried = jnp.dot(c_block, start.astype(BF16), preferred_element_type=F32)
                out_ref[rows, columns] = grown * carried
        copies[c].wait()
        gram = lax.dot_general(
            c_block, b_ref[rows, :], (((1,), (1,)), ((), ())), preferred_element_type=F32
        )
        gram_00 = jnp.where(lower, gram[:half, :half], 0.0)
        gram_10 = gram[half:, :half]
        gram_11 = jnp.where(lower, gram[half:, half:], 0.0)
        for h in range(head_count):
            columns = slice(h * HEAD_DIM, (h + 1) * HEAD_DIM)
            rise = jnp.broadcast_to(q_block[:, h : h + 1], (BLOCK, half))
            fall = brow_ref[h : h + 1, rows]
            step = brow_ref[SLOT + h : SLOT + h + 1, rows]
            w_00 = gram_00 * jnp.exp2(jnp.minimum(rise[:half] - fall[:, :half], 120.0))
            w_10 = gram_10 * jnp.exp2(rise[half:] - fall[:, :half])
            w_11 = gram_11 * jnp.exp2(jnp.minimum(rise[half:] - fall[:, half:], 120.0))
            w_00 = w_00 * step[:, :half]
            w_10 = w_10 * step[:, :half]
            w_11 = w_11 * step[:, half:]
            x_head = held[c, :, columns]
            top = jnp.dot(w_00.astype(BF16), x_head[:half], preferred_element_type=F32)
            low = jnp.concatenate([w_10.astype(BF16), w_11.astype(BF16)], axis=1)
            bottom = jnp.dot(low, x_head, preferred_element_type=F32)
            skip = dec_ref[2 * block_count + 1 : 2 * block_count + 2, columns] * x_head.astype(F32)
            own = jnp.concatenate([top, bottom], axis=0) + skip
            if c > 0:
                own = own + out_ref[rows, columns]
            out_ref[rows, columns] = own

    z_copy.wait()


def inner(c_act, b_act, x, z, q, brow, starts, state, dec):
    length, width = x.shape
    return pl.pallas_call(
        inner_kernel,
        out_shape=[kept_in_vmem((length, width), F32), kept_in_vmem(z.shape, z.dtype)],
        in_specs=[whole()] * 2 + [whole(pltpu.HBM)] * 2 + [whole()] * 5,
        out_specs=[whole()] * 2,
        scratch_shapes=[
            pltpu.VMEM((128, width), BF16),
            pltpu.VMEM((length // BLOCK, BLOCK, width), BF16),
            pltpu.SemaphoreType.DMA((length // BLOCK,)),
            pltpu.SemaphoreType.DMA,
        ],
        compiler_params=params(),
        cost_estimate=cost(0, 80 * length * width),
    )(c_act, b_act, x, z, q, brow, starts, state, dec)


def gate_kernel(second, at_ref, c_ref, y_ref, z_ref, q_ref, in_ref, *refs):
    out_ref, sum_ref, expand_ref, squares_ref = refs[-4:]
    width = in_ref.shape[1]
    base = pl.multiple_of(width - at_ref[1] if second else at_ref[1], 128)
    expander(expand_ref, 5, base)
    blocks = [slice(c, c + BLOCK) for c in range(0, y_ref.shape[0], BLOCK)]
    for rows in blocks:
        c_block = c_ref[rows, :]
        q_short = q_ref[rows, :].astype(BF16)
        squares = None
        for part in tiles(width, 256):
            size = part.stop - part.start
            columns = pl.ds(pl.multiple_of(base + part.start, 128), size)
            grown = jnp.dot(q_short, expand_ref[:, part], preferred_element_type=F32)
            carried = jnp.dot(c_block, in_ref[:, part], preferred_element_type=F32)
            gated = (y_ref[rows, columns] + grown * carried) * silu(z_ref[rows, columns].astype(F32))
            out_ref[rows, columns] = gated
            square = gated * gated
            for i in range(0, size, 128):
                one = square[:, i : i + 128]
                squares = one if squares is None else squares + one
        squares_ref[rows, :] = squares
    for rows in blocks:
        total = jnp.sum(squares_ref[rows, :].T, axis=0, keepdims=True)
        sum_ref[:, rows] = refs[0][:, rows] + total if second else total


def gate(at, c_act, y, z, q, incoming, *before):
    length, width = y.shape
    return pl.pallas_call(
        functools.partial(gate_kernel, len(before) > 0),
        out_shape=[
            kept_in_vmem((length, width), F32),
            kept_in_vmem((1, length), F32),
        ],
        in_specs=[whole(pltpu.SMEM)] + [whole()] * (5 + len(before)),
        out_specs=[whole()] * 2,
        scratch_shapes=[
            pltpu.VMEM((128, incoming.shape[1]), BF16),
            pltpu.VMEM((length, 128), F32),
        ],
        input_output_aliases={2: 0},
        compiler_params=params(),
        cost_estimate=cost(0, 8 * length * width),
    )(at, c_act, y, z, q, incoming, *before)


def norm_kernel(g_ref, one_ref, two_ref, gain_ref, out_ref, held, sems):
    copies = []
    for c in range(g_ref.shape[0] // BLOCK):
        rows = slice(c * BLOCK, (c + 1) * BLOCK)
        square_sum = one_ref[:, rows] + two_ref[:, rows]
        inverse = lax.rsqrt(square_sum / INNER + 1e-05)
        scale = jnp.broadcast_to(inverse, (128, BLOCK)).T
        for i in range(0, g_ref.shape[1], 128):
            columns = slice(i, i + 128)
            held[c, :, columns] = (g_ref[rows, columns] * scale * gain_ref[:, columns]).astype(BF16)
        copy = pltpu.make_async_copy(held.at[c], out_ref.at[rows, :], sems.at[c])
        copy.start()
        copies.append(copy)
    for copy in copies:
        copy.wait()


def norm(gated, one, two, gain):
    length, width = gated.shape
    count = length // BLOCK
    return pl.pallas_call(
        norm_kernel,
        out_shape=jax.ShapeDtypeStruct((length, width), BF16),
        in_specs=[whole()] * 4,
        out_specs=whole(pltpu.HBM),
        scratch_shapes=[
            pltpu.VMEM((count, BLOCK, width), BF16),
            pltpu.SemaphoreType.DMA((count,)),
        ],
        compiler_params=params(),
        cost_estimate=cost(0, 0),
    )(gated, one, two, gain)


SWAP = [(0, 1), (1, 0), (2, 3), (3, 2)]


def zone_swap(a, k):
    size = lax.axis_size("head")
    return lax.ppermute(a, "head", [(i, i ^ (2 * k)) for i in range(size)])


def side_swap(a):
    size = lax.axis_size("head")
    return lax.ppermute(a, "head", [(i, i ^ 1) for i in range(size)])


def chained_state(at, kept, sent, own, after, late):
    size = lax.axis_size("seq")
    if size == 4:
        got = [lax.ppermute(piece, "seq", SWAP) for piece in sent]
        both, got, partner = meet(at, kept, own, got, late)
        crossed = lax.ppermute(both, "seq", [(0, 2), (1, 3)])
        mine, passed = arrive(at, crossed, kept, got, own, partner, after)
        return mine, lax.ppermute(passed, "seq", SWAP)
    totals = lax.all_gather(jnp.concatenate([kept, *[a[:STATE] for a in sent]], axis=1), "seq")
    decays = lax.all_gather(own, "seq")

    def one(hop, state):
        decay = lax.dynamic_index_in_dim(decays, hop, 0, False)
        return decay * state + lax.dynamic_index_in_dim(totals, hop, 0, False).astype(F32)

    place = lax.axis_index("seq")
    state = lax.fori_loop(0, place, one, jnp.zeros(totals.shape[1:], F32)).astype(BF16)
    half = kept.shape[1]
    return state[:, :half], state[:, half:]


def on_device(x_inner, z_gate, bc_raw, conv_weight, conv_bias, dt_raw, a_log, d_skip, norm_gain):
    x_inner, z_gate = in_hbm(x_inner), in_hbm(z_gate)
    head_count = a_log.shape[0]
    own_rows = bc_raw.shape[0]
    seq_size = lax.axis_size("seq")
    shifts = range(1, lax.axis_size("head") // 2)
    width = x_inner.shape[1]
    first_channel = 0
    if seq_size == 4:
        first_channel = (1 - lax.rem(lax.axis_index("seq"), 2)) * (width // 2)
    place = jnp.stack([lax.axis_index("head"), first_channel]).astype(jnp.int32)
    own_b, own_c, place = prepare(place, bc_raw)
    zones_b = [zone_swap(own_b, k) for k in shifts]
    side_b = side_swap(own_b)
    pad = SLOT - head_count
    q, brow, dec, own_decay, xs_first, xs_later = rates(
        jnp.pad(dt_raw.T, ((0, pad), (0, 0))),
        jnp.pad(a_log, (0, pad))[None, :],
        jnp.pad(d_skip, (0, pad))[None, :],
        x_inner,
    )
    side_c = side_swap(own_c)
    cat_b, pair_c = pack(zones_b, own_c, side_c, xs_first, side_b)
    others_b = side_swap(cat_b)
    pairs_c = [zone_swap(pair_c, k) for k in shifts]
    per = own_b.shape[0]
    sources_b = [own_b, side_b, *zones_b, others_b]
    plan_b = [(0, 0, False, 0), (1, 0, True, 0)]
    plan_b += [(k + 1, 0, False, k) for k in shifts]
    plan_b += [(len(zones_b) + 2, (k - 1) * per, True, k) for k in shifts]
    sources_c = [pair_c, *pairs_c]
    plan_c = [(k, 0, False, k) for k in range(len(sources_c))]
    plan_c += [(k, own_rows, True, k) for k in range(len(sources_c))]
    bias = conv_bias[None, :]
    b_act, first_b, last_rows = activate(
        place, sources_b, plan_b, True, conv_weight, bias, own_rows, [xs_first]
    )
    rims = lax.ppermute(last_rows, "seq", [(i, i + 1) for i in range(seq_size - 1)])
    starts, later = later_states(b_act, xs_later, dec)
    b_act, state_0, kept, *sent = first_state(
        place, b_act, first_b, rims, conv_weight, bias, xs_first, dec, later, own_decay
    )
    c_act, _, _ = activate(place, [*sources_c, rims], plan_c, False, conv_weight, bias, own_rows)
    local, z_held = inner(c_act, b_act, x_inner, z_gate, q, brow, starts, state_0, dec)
    state_one, state_two = chained_state(place, kept, sent, own_decay, local, pairs_c)
    gated, square_one = gate(place, c_act, local, z_held, q, state_one)
    gated, square_sum = gate(place, c_act, gated, z_held, q, state_two, square_one)
    column = sum([zone_swap(square_sum, k) for k in shifts], square_sum)
    return norm(gated, column, side_swap(column), norm_gain[None, :])


def solution(mesh):
    placed = (
        P("seq", "head"),
        P("seq", "head"),
        P(("seq", "head"), None),
        P(),
        P(),
        P("seq", "head"),
        P("head"),
        P("head"),
        P("head"),
    )
    return jax.shard_map(
        on_device, mesh=mesh, in_specs=placed, out_specs=P("seq", "head"), check_vma=False
    )
```
